32 devices in a mesh: frame: 8 (over z, x), head: 4 (over y, core).
Axes of the slice: x: 2, y: 2, z: 4, core: 2. Of those that a mesh axis runs over, the one named last changes fastest.
Arguments:
- queries: bfloat16 [2048, 5120], P('frame', 'head'), may hold values from -20 to 20
- key_vectors: bfloat16 [2048, 5120], P('frame', 'head'), may hold values from -20 to 20
- value_vectors: bfloat16 [2048, 5120], P('frame', 'head'), may hold values from -6 to 6
- live_blocks: int32 [32, 32], P('frame'), may hold values from 0 to 1, as said below
- out_weight: bfloat16 [5120, 5120], P('head'), may hold values from -0.078125 to 0.078125
Outputs:
- mixed: bfloat16 [2048, 5120], P('frame', 'head')
The draws below stay inside these ranges and needn't reach their ends.
Inputs may be any that keep to these rules, and one draw needn't show every extreme that they name: live_blocks is 1 wherever the distance |i - j| between the frames i, j of the query block and the key block is 0 or 1, and 0 wherever that distance is not 0, 1 or a power of two up to 4.
All inputs are finite; a program needn't handle non-finite values.
Results may differ from the reference program's by a relative error of at most 0.015.
Values may be sent and summed in bfloat16 or wider, within the bound.
No kernel may reach another device: no remote copies, remote signals or barrier semaphores. Data moves between devices by JAX's collectives and lax.ppermute only.
A program may use at most 192 MiB of HBM per device.

```python
import jax
import jax.numpy as jnp
from jax import lax

HEADS = 40
HDIM = 128
D = 5120
FRAME_TOK = 256
BLK = 64
TOKENS = 2048
N_FRAME = 8
N_HEAD = 4


def draw_key_vectors(key, part):
    key = jax.random.fold_in(key, 11)
    drawn = jnp.clip(jax.random.normal(key, (TOKENS, D), jnp.float32), -6.0, 6.0)
    return drawn.astype(jnp.bfloat16)


def draw_queries(key, part):
    key = jax.random.fold_in(key, 12)
    drawn = jnp.clip(jax.random.normal(key, (TOKENS, D), jnp.float32), -6.0, 6.0)
    return drawn.astype(jnp.bfloat16)


def draw_live_blocks(key, part):
    key = jax.random.fold_in(key, 5)
    blocks = FRAME_TOK // BLK
    count = TOKENS // BLK
    query_frame = jnp.arange(count, dtype=jnp.int32) // blocks
    key_frame = jnp.arange(count, dtype=jnp.int32) // blocks
    distance = jnp.abs(key_frame[None, :] - query_frame[:, None])
    power = (distance >= 2) & (distance <= N_FRAME // 2) & (distance & distance - 1 == 0)
    frame_weight = jax.random.randint(jax.random.fold_in(key, 1), (N_FRAME,), 1, 3)[query_frame]
    draws = jax.random.randint(jax.random.fold_in(key, 2), (count, count), 0, 1 << 20)
    picked = draws % jnp.maximum(distance, 1) < frame_weight[:, None]
    live = jnp.where(distance <= 1, 1, jnp.where(power & picked, 1, 0))
    return live.astype(jnp.int32)


def block_scale(own_key, extent, pieces, smallest, largest):
    def one(dim, parts):
        steps = jax.random.uniform(jax.random.fold_in(jax.random.fold_in(own_key, 6), dim), (parts,), jnp.float32, smallest / len(pieces), largest / len(pieces))
        return jnp.repeat(jnp.exp(steps), extent[dim] // parts).reshape((-1,) + (1,) * (len(extent) - dim - 1))

    loudness = one(*pieces[0])
    for cut in pieces[1:]:
        loudness = loudness * one(*cut)
    return loudness


def scatter_about(key, shape, scale, reach, shards=(), kind=jnp.bfloat16):
    entries = scale * jax.random.normal(key, shape, jnp.float32)
    if shards:
        entries = entries * block_scale(key, shape, shards, -0.22, 0.18)
    return jnp.clip(entries, -reach, reach).astype(kind)


def setup_inputs(seed: int = 0) -> dict:
    arg_keys = jax.random.split(jax.random.key(seed), 6)
    return {
        "queries": draw_queries(jax.random.fold_in(arg_keys[5], 71), 0),
        "key_vectors": draw_key_vectors(jax.random.fold_in(arg_keys[5], 71), 0),
        "value_vectors": scatter_about(arg_keys[2], (TOKENS, D), 1.0, 6.0, ((0, 8), (1, 4))),
        "live_blocks": draw_live_blocks(jax.random.fold_in(arg_keys[5], 71), 0),
        "out_weight": scatter_about(arg_keys[4], (D, D), D ** -0.5, 0.078125, ((0, 4),)),
    }


def offsets_for(frames):
    result = [0]
    step = 1
    while step <= frames // 2:
        result.append(step)
        result.append(-step)
        step = step * 2
    return result


def reference(queries, key_vectors, value_vectors, live_blocks, out_weight):
    blocks = FRAME_TOK // BLK
    offsets = offsets_for(N_FRAME)
    scale = 1.0 / (HDIM ** 0.5)
    query_heads = queries.reshape(N_FRAME, FRAME_TOK, HEADS, HDIM)
    key_heads = key_vectors.reshape(N_FRAME, FRAME_TOK, HEADS, HDIM)
    value_heads = value_vectors.reshape(N_FRAME, FRAME_TOK, HEADS, HDIM)
    live_grid = live_blocks.reshape(N_FRAME, blocks, N_FRAME, blocks)

    def one_frame(frame):
        key_list = []
        value_list = []
        mask_list = []
        own_live = lax.dynamic_index_in_dim(live_grid, frame, 0, False)
        for offset in offsets:
            target = (frame + offset).astype(jnp.int32)
            inside = (target >= 0) & (target < N_FRAME)
            other = jnp.clip(target, 0, N_FRAME - 1).astype(jnp.int32)
            key_list.append(lax.dynamic_index_in_dim(key_heads, other, 0, False))
            value_list.append(lax.dynamic_index_in_dim(value_heads, other, 0, False))
            square = lax.dynamic_index_in_dim(own_live, other, 1, False)
            square = jnp.where(inside, square, 0)
            mask_list.append(jnp.repeat(jnp.repeat(square, BLK, 0), BLK, 1))
        key_all = jnp.concatenate(key_list, 0).astype(jnp.float32)
        value_all = jnp.concatenate(value_list, 0).astype(jnp.float32)
        mask_all = jnp.concatenate(mask_list, 1)
        query_now = lax.dynamic_index_in_dim(query_heads, frame, 0, False).astype(jnp.float32)
        scores = jnp.einsum("qhd,khd->hqk", query_now, key_all) * scale
        scores = jnp.where(mask_all[None] > 0, scores, -jnp.inf)
        peak = jnp.max(scores, axis=2, keepdims=True)
        expo = jnp.exp(scores - peak)
        total = jnp.sum(expo, axis=2, keepdims=True)
        weights = (expo / total).astype(jnp.bfloat16).astype(jnp.float32)
        attended = jnp.einsum("hqk,khd->qhd", weights, value_all).astype(jnp.bfloat16)
        return attended.reshape(FRAME_TOK, D)

    attended = lax.map(one_frame, jnp.arange(N_FRAME, dtype=jnp.int32)).reshape(TOKENS, D)
    width = D // N_HEAD
    summed = jnp.zeros((TOKENS, D), jnp.float32)
    for group in range(N_HEAD):
        partial_g = jnp.dot(attended[:, group * width:(group + 1) * width], out_weight[group * width:(group + 1) * width, :], preferred_element_type=jnp.float32).astype(jnp.bfloat16)
        partial_g = lax.optimization_barrier(partial_g)
        summed = summed + partial_g.astype(jnp.float32)
    return summed.astype(jnp.bfloat16)
```

```python
import functools
import math

import jax
import jax.numpy as jnp
from jax import lax
from jax.experimental import pallas as pl
from jax.experimental.pallas import tpu as pltpu
from jax.sharding import PartitionSpec as P

HDIM = 128
BLK = 64
EXP_SCALE = math.log2(math.e) / math.sqrt(HDIM)
DEAD = -1e30
CHUNKS = (4, 3, 3)
F32 = jnp.float32
BF16 = jnp.bfloat16


def offsets_for(frames):
    result = [0]
    step = 1
    while step <= frames // 2:
        result.append(step)
        result.append(-step)
        step = step * 2
    return result


def shift(frames, by, keep=None):
    return [
        (i, i + by)
        for i in range(frames)
        if 0 <= i + by < frames and (keep is None or keep(i))
    ]


def params(megabytes=48):
    return pltpu.CompilerParams(vmem_limit_bytes=megabytes << 20)


def pack_kernel(starts, widths, k_ref, v_ref, *rest):
    outs, sem = rest[:-1], rest[-1]
    rows = k_ref.shape[0]
    copies = []
    for n, out in enumerate(outs):
        columns = pl.ds(starts[n], widths[n])
        for half, ref in enumerate((k_ref, v_ref)):
            copies.append(
                pltpu.make_async_copy(
                    ref.at[:, columns], out.at[pl.ds(half * rows, rows), :], sem.at[2 * n + half]
                )
            )
    for copy in copies:
        copy.start()
    for copy in copies:
        copy.wait()


def pack(keys, values, starts, widths):
    rows = keys.shape[0]
    moved = 4 * rows * sum(widths) * 2
    return pl.pallas_call(
        functools.partial(pack_kernel, starts, widths),
        out_shape=[jax.ShapeDtypeStruct((2 * rows, w), BF16) for w in widths],
        in_specs=[pl.BlockSpec(memory_space=pl.ANY)] * 2,
        out_specs=[pl.BlockSpec(memory_space=pl.ANY)] * len(widths),
        scratch_shapes=[pltpu.SemaphoreType.DMA((2 * len(widths),))],
        cost_estimate=pl.CostEstimate(flops=0, bytes_accessed=moved, transcendentals=0),
        name="pack",
    )(keys, values)


def attend_kernel(groups, flag_ref, q_ref, k_ref, v_ref, bias_ref, *rest):
    slots, o_ref = rest[:-1], rest[-1]
    rows = q_ref.shape[0]
    q = q_ref[...]
    scores = []
    values = []
    for n in range(len(groups) + 1):
        if n == 0:
            key, value = k_ref[...], v_ref[...]
        elif len(groups[n - 1]) == 1:
            ref = slots[groups[n - 1][0]]
            key, value = ref[:rows, :], ref[rows:, :]
        else:
            one, two = (slots[g] for g in groups[n - 1])
            first = flag_ref[n] > 0
            both = jnp.where(first, one[...], two[...])
            key, value = both[:rows, :], both[rows:, :]
        s = lax.dot_general(q, key, (((1,), (1,)), ((), ())), preferred_element_type=F32)
        bias = jnp.concatenate(
            [
                jnp.broadcast_to(bias_ref[b : b + 1, n * rows : (n + 1) * rows], (BLK, rows))
                for b in range(rows // BLK)
            ],
            0,
        )
        scores.append(s + bias)
        values.append(value)
    peak = functools.reduce(jnp.maximum, scores)
    peak = jnp.max(peak, axis=1, keepdims=True)
    acc = None
    total = None
    for s, value in zip(scores, values):
        e = jnp.exp2((s - peak) * EXP_SCALE)
        total = e if total is None else total + e
        part = jnp.dot(e.astype(BF16), value, preferred_element_type=F32)
        acc = part if acc is None else acc + part
    total = jnp.sum(total, axis=1, keepdims=True)
    o_ref[...] = (acc / total).astype(o_ref.dtype)


def attend(queries, keys, values, bias, flags, slots, groups, first, heads):
    rows = queries.shape[0]
    wide = lambda h, f: (0, first + h)
    near = lambda h, f: (0, h)
    keys_seen = rows * (len(groups) + 1)
    return pl.pallas_call(
        functools.partial(attend_kernel, groups),
        out_shape=jax.ShapeDtypeStruct((rows, heads * HDIM), BF16),
        grid_spec=pltpu.PrefetchScalarGridSpec(
            num_scalar_prefetch=1,
            grid=(heads,),
            in_specs=[pl.BlockSpec((rows, HDIM), wide)] * 3
            + [pl.BlockSpec(bias.shape, lambda h, f: (0, 0))]
            + [pl.BlockSpec((2 * rows, HDIM), near)] * len(slots),
            out_specs=pl.BlockSpec((rows, HDIM), near),
        ),
        compiler_params=params(),
        cost_estimate=pl.CostEstimate(
            flops=4 * heads * rows * keys_seen * HDIM,
            bytes_accessed=4 * heads * keys_seen * HDIM,
            transcendentals=heads * rows * keys_seen,
        ),
        name="attend",
    )(flags, queries, keys, values, bias, *slots)


def project_kernel(count, pick_ref, *refs):
    weight, outs = refs[count], refs[count + 1]
    acc = None
    at = 0
    for ref in refs[:count]:
        a = ref[...]
        part = jnp.dot(a, weight[at : at + a.shape[1], :], preferred_element_type=F32)
        at += a.shape[1]
        acc = part if acc is None else acc + part
    outs[...] = acc.astype(outs.dtype)


def project(pieces, weight, picks, rows_used, tile):
    rows = pieces[0].shape[0]
    columns = weight.shape[1] // lax.axis_size("head")
    steps = columns // tile
    groups = picks.shape[0]
    return pl.pallas_call(
        functools.partial(project_kernel, len(pieces)),
        out_shape=jax.ShapeDtypeStruct((groups * rows, columns), BF16),
        grid_spec=pltpu.PrefetchScalarGridSpec(
            num_scalar_prefetch=1,
            grid=(groups, steps),
            in_specs=[pl.BlockSpec(p.shape, lambda g, t, k: (0, 0)) for p in pieces]
            + [pl.BlockSpec((rows_used, tile), lambda g, t, k: (0, k[g] * steps + t))],
            out_specs=pl.BlockSpec((rows, tile), lambda g, t, k: (g, t)),
        ),
        compiler_params=params(),
        cost_estimate=pl.CostEstimate(
            flops=2 * rows * rows_used * columns * groups,
            bytes_accessed=2 * rows_used * columns * groups,
            transcendentals=0,
        ),
        name="project",
    )(picks, *pieces, weight)


def finish_kernel(count, *refs):
    out = refs[-1]
    acc = None
    for a, w in zip(refs[:count], refs[count : 2 * count]):
        part = jnp.dot(a[...], w[...], preferred_element_type=F32)
        acc = part if acc is None else acc + part
    for ref in refs[2 * count : -1]:
        acc = acc + ref[...].astype(F32)
    out[...] = acc.astype(out.dtype)


def finish(pieces, weights, sums, tile):
    rows = pieces[0].shape[0]
    columns = weights[0].shape[1]
    depth = weights[0].shape[0]
    return pl.pallas_call(
        functools.partial(finish_kernel, len(pieces)),
        out_shape=jax.ShapeDtypeStruct((rows, columns), BF16),
        grid=(columns // tile,),
        in_specs=[pl.BlockSpec(p.shape, lambda t: (0, 0)) for p in pieces]
        + [pl.BlockSpec((depth, tile), lambda t: (0, t))] * len(weights)
        + [pl.BlockSpec((rows, tile), lambda t: (0, t))] * len(sums),
        out_specs=pl.BlockSpec((rows, tile), lambda t: (0, t)),
        compiler_params=params(),
        cost_estimate=pl.CostEstimate(
            flops=2 * rows * depth * columns * len(pieces),
            bytes_accessed=2 * depth * columns * len(pieces),
            transcendentals=0,
        ),
        name="finish",
    )(*pieces, *weights, *sums)


def send(x, axis, pairs):
    return lax.ppermute(x, axis, pairs)


def first_hops(kv, frames):
    if frames != 8:
        return [send(kv, "frame", shift(frames, -o)) for o in offsets_for(frames)[1:]]
    return [
        send(kv, "frame", [(i, i ^ 1) for i in range(frames)]),
        send(kv, "frame", shift(frames, 2)),
        send(kv, "frame", shift(frames, -2)),
    ]


def second_hops(hops, frames):
    if frames != 8:
        return hops
    pair, low, high = hops
    inner = lambda i: 2 <= i <= 5
    return hops + [
        send(low, "frame", shift(frames, -1, lambda i: i % 2 == 1 and i >= 2)),
        send(high, "frame", shift(frames, 1, lambda i: i % 2 == 0 and i <= 5)),
        send(low, "frame", shift(frames, 2, inner)),
        send(high, "frame", shift(frames, -2, inner)),
    ]


def plan(frames, own):
    if frames != 8:
        offsets = offsets_for(frames)
        groups = tuple((n,) for n in range(len(offsets) - 1))
        return groups, [own + o for o in offsets], [jnp.int32(1)] * len(offsets)
    even = own % 2 == 0
    upper = own >= 4
    groups = ((0,), (1,), (2,), (3, 4), (5, 6))
    one = jnp.int32(1)
    held = [
        own,
        jnp.where(even, own + 1, own - 1),
        own - 2,
        own + 2,
        jnp.where(even, own - 1, own + 1),
        jnp.where(upper, own - 4, own + 4),
    ]
    return groups, held, [one, one, one, one, even.astype(jnp.int32), upper.astype(jnp.int32)]


def on_device(queries, key_vectors, value_vectors, live_blocks, out_weight):
    frames = lax.axis_size("frame")
    own = lax.axis_index("frame")
    group = lax.axis_index("head")
    rows = queries.shape[0]
    blocks = rows // BLK
    columns = out_weight.shape[1] // lax.axis_size("head")

    widths = [c * HDIM for c in CHUNKS]
    starts = [sum(widths[:n]) for n in range(len(widths))]
    packed = pack(key_vectors, value_vectors, starts[:1], widths[:1]) + pack(
        key_vectors, value_vectors, starts[1:], widths[1:]
    )
    hops = [first_hops(kv, frames) for kv in packed]

    groups, held, flags = plan(frames, own)
    flags = jnp.stack(flags)
    lives = []
    for frame in held:
        inside = (frame >= 0) & (frame < frames)
        square = lax.dynamic_slice_in_dim(
            live_blocks, jnp.clip(frame, 0, frames - 1) * blocks, blocks, 1
        )
        lives.append(jnp.where(inside, square, 0))
    live = jnp.repeat(jnp.concatenate(lives, 1), BLK, 1)
    bias = jnp.where(live > 0, 0.0, DEAD).astype(F32)

    last = starts[-1]

    def weight_part(other):
        return lax.dynamic_slice(
            out_weight, (jnp.int32(last), other * columns), (widths[-1], columns)
        )

    swap = lambda x, bit: send(x, "head", [(g, g ^ bit) for g in range(4)])
    late_weights = [weight_part(group)] + [
        swap(weight_part(group ^ bit), bit) for bit in (1, 2, 3)
    ]

    attended = []
    for n, width in enumerate(widths):
        slots = second_hops(hops[n], frames)
        attended.append(
            attend(
                queries, key_vectors, value_vectors, bias, flags, slots, groups,
                starts[n] // HDIM, width // HDIM,
            )
        )

    early = attended[:-1]
    away = project(early, out_weight, jnp.stack([group ^ 3, group ^ 2]), last, columns // 2)
    near = project(early, out_weight, jnp.stack([group ^ 1, group]), last, columns // 2)
    crossed = (away[rows:].astype(F32) + swap(away[:rows], 1).astype(F32)).astype(BF16)
    from_far = swap(crossed, 2)
    from_near = swap(near[:rows], 1)

    late = attended[-1]
    pieces = [late] + [swap(late, bit) for bit in (1, 2, 3)]
    return finish(pieces, late_weights, [near[rows:], from_near, from_far], columns // 2)


def solution(mesh):
    placed = (
        P("frame", "head"),
        P("frame", "head"),
        P("frame", "head"),
        P("frame", None),
        P("head", None),
    )
    return jax.shard_map(
        on_device, mesh=mesh, in_specs=placed, out_specs=P("frame", "head"), check_vma=False
    )
```

```python
import functools
import math

import jax
import jax.numpy as jnp
from jax import lax
from jax.experimental import pallas as pl
from jax.experimental.pallas import tpu as pltpu
from jax.sharding import PartitionSpec as P

HDIM = 128
BLK = 64
EXP_SCALE = math.log2(math.e) / math.sqrt(HDIM)
DEAD = -1e30
F32 = jnp.float32
BF16 = jnp.bfloat16


def offsets_for(frames):
    result = [0]
    step = 1
    while step <= frames // 2:
        result.append(step)
        result.append(-step)
        step = step * 2
    return result


def params(megabytes=56):
    return pltpu.CompilerParams(vmem_limit_bytes=megabytes << 20)


def send(x, axis, pairs):
    return lax.ppermute(x, axis, pairs)


def from_offset(x, frames, offset):
    return send(
        x, "frame", [(i + offset, i) for i in range(frames) if 0 <= i + offset < frames]
    )


def early_hops(x, frames):
    if frames != 8:
        return [from_offset(x, frames, o) for o in offsets_for(frames)[1:-2]]
    return [
        send(x, "frame", [(i, i ^ 2) for i in range(frames)]),
        send(x, "frame", [(i, i ^ 6) for i in (2, 3, 4, 5)]),
        send(x, "frame", [(i, i ^ 1) for i in range(frames)]),
    ]


def late_hops(x, hops, own, frames):
    if frames != 8:
        return [from_offset(x, frames, o) for o in offsets_for(frames)[-2:]]
    outer, inner, _ = hops
    across = jnp.where((own == 2) | (own == 5), inner, outer)
    return [
        send(outer, "frame", [(i, i ^ 6) for i in (2, 3, 4, 5)]),
        send(inner, "frame", [(i, i ^ 2) for i in (2, 3, 4, 5)]),
        send(across, "frame", [(i, i ^ 1) for i in (0, 2, 3, 4, 5, 7)]),
    ]


def plan(own, frames):
    if frames != 8:
        held = [own + o for o in offsets_for(frames)]
        return held[:-2], held[-2:], ((0,), (1,)), jnp.int32(0)
    middle = (own >= 2) & (own <= 5)
    even = own % 2 == 0
    early = [own, own ^ 2, jnp.where(middle, own ^ 6, -1), own ^ 1]
    late = [own ^ 4, jnp.where(even, own - 1, own + 1)]
    return early, late, ((0, 1), (2,)), middle.astype(jnp.int32)


def bias_of(held, live_blocks, frames, rows):
    blocks = rows // BLK
    lives = []
    for frame in held:
        inside = (frame >= 0) & (frame < frames)
        square = lax.dynamic_slice_in_dim(
            live_blocks, jnp.clip(frame, 0, frames - 1) * blocks, blocks, 1
        )
        lives.append(jnp.where(inside, square, 0))
    live = jnp.repeat(jnp.concatenate(lives, 1), BLK, 1)
    return jnp.where(live > 0, 0.0, DEAD).astype(F32)


def scores_of(q, key, bias_ref, n):
    rows = q.shape[0]
    s = lax.dot_general(q, key, (((1,), (1,)), ((), ())), preferred_element_type=F32)
    bias = [
        jnp.broadcast_to(bias_ref[b : b + 1, n * rows : (n + 1) * rows], (BLK, rows))
        for b in range(rows // BLK)
    ]
    return s + jnp.concatenate(bias, 0)


def early_kernel(count, q_ref, k_ref, v_ref, bias_ref, *rest):
    keys, values = rest[:count], rest[count : 2 * count]
    sum_ref, peak_ref, total_ref = rest[2 * count :]
    q = q_ref[...]
    scores = [lax.dot_general(q, k_ref[...], (((1,), (1,)), ((), ())), preferred_element_type=F32)]
    for n, ref in enumerate(keys):
        scores.append(scores_of(q, ref[...], bias_ref, n))
    peak = jnp.max(functools.reduce(jnp.maximum, scores), axis=1, keepdims=True)
    acc = None
    total = None
    for s, ref in zip(scores, [v_ref, *values]):
        e = jnp.exp2((s - peak) * EXP_SCALE)
        total = e if total is None else total + e
        part = jnp.dot(e.astype(BF16), ref[...], preferred_element_type=F32)
        acc = part if acc is None else acc + part
    total = jnp.sum(total, axis=1, keepdims=True)
    sum_ref[...] = acc
    peak_ref[...] = jnp.broadcast_to(peak, peak_ref.shape)
    total_ref[...] = jnp.broadcast_to(total, total_ref.shape)


def early_attention(queries, keys, values, bias, early_keys, early_values):
    rows, width = queries.shape
    head = pl.BlockSpec((rows, HDIM), lambda h: (0, h))
    count = len(early_keys)
    seen = rows * (count + 1)
    heads = width // HDIM
    return pl.pallas_call(
        functools.partial(early_kernel, count),
        out_shape=[jax.ShapeDtypeStruct((rows, width), F32)] * 3,
        grid=(heads,),
        in_specs=[head] * 3
        + [pl.BlockSpec(bias.shape, lambda h: (0, 0))]
        + [head] * (2 * count),
        out_specs=[head] * 3,
        compiler_params=params(),
        cost_estimate=pl.CostEstimate(
            flops=4 * heads * rows * seen * HDIM,
            bytes_accessed=4 * heads * seen * HDIM,
            transcendentals=heads * rows * seen,
        ),
        name="early_attention",
    )(queries, keys, values, bias, *early_keys, *early_values)


def pick(refs, group, flag_ref):
    if len(group) == 1:
        return refs[group[0]][...]
    one, two = (refs[g][...] for g in group)
    return jnp.where(flag_ref[0] > 0, one, two)


def late_kernel(groups, flag_ref, q_ref, bias_ref, sum_ref, peak_ref, total_ref, *rest):
    keys, weight_ref, scaled_ref = rest[:-2], rest[-2], rest[-1]
    q = q_ref[...]
    rows = q.shape[0]
    scores = [
        scores_of(q, pick(keys, group, flag_ref), bias_ref, n) for n, group in enumerate(groups)
    ]
    before = peak_ref[...]
    peak = jnp.max(functools.reduce(jnp.maximum, scores), axis=1, keepdims=True)
    peak = jnp.maximum(before[:, :1], peak)
    expos = [jnp.exp2((s - peak) * EXP_SCALE) for s in scores]
    total = jnp.sum(functools.reduce(jnp.add, expos), axis=1, keepdims=True)
    shrink = jnp.exp2((before[:, :1] - peak) * EXP_SCALE)
    total = total_ref[...][:, :1] * shrink + total
    over = 1.0 / total
    for n, e in enumerate(expos):
        weight_ref[:, n * rows : (n + 1) * rows] = (e * over).astype(BF16)
    scaled_ref[...] = sum_ref[...] * (shrink * over)


def late_weights(queries, bias, sums, peaks, totals, late_keys, groups, flag):
    rows, width = queries.shape
    head = pl.BlockSpec((rows, HDIM), lambda h, f: (0, h))
    heads = width // HDIM
    seen = rows * len(groups)
    return pl.pallas_call(
        functools.partial(late_kernel, groups),
        out_shape=[
            jax.ShapeDtypeStruct((rows, heads * seen), BF16),
            jax.ShapeDtypeStruct((rows, width), F32),
        ],
        grid_spec=pltpu.PrefetchScalarGridSpec(
            num_scalar_prefetch=1,
            grid=(heads,),
            in_specs=[head]
            + [pl.BlockSpec(bias.shape, lambda h, f: (0, 0))]
            + [head] * (3 + len(late_keys)),
            out_specs=[pl.BlockSpec((rows, seen), lambda h, f: (0, h)), head],
        ),
        compiler_params=params(),
        cost_estimate=pl.CostEstimate(
            flops=2 * heads * rows * seen * HDIM,
            bytes_accessed=4 * heads * seen * HDIM,
            transcendentals=heads * rows * seen,
        ),
        name="late_weights",
    )(flag, queries, bias, sums, peaks, totals, *late_keys)


def first_project_kernel(groups, count, flag_ref, pick_ref, scaled_ref, weights_ref, *rest):
    values = rest[:count]
    w_ref, out_ref, att_ref = rest[count:]
    rows, width = scaled_ref.shape
    seen = rows * len(groups)

    @pl.when((pl.program_id(0) == 0) & (pl.program_id(1) == 0))
    def _():
        for h in range(width // HDIM):
            columns = slice(h * HDIM, (h + 1) * HDIM)
            acc = scaled_ref[:, columns]
            for n, group in enumerate(groups):
                value = pick([ref.at[:, columns] for ref in values], group, flag_ref)
                weight = weights_ref[:, h * seen + n * rows : h * seen + (n + 1) * rows]
                acc += jnp.dot(weight, value, preferred_element_type=F32)
            att_ref[:, columns] = acc.astype(BF16)

    out_ref[...] = jnp.dot(att_ref[...], w_ref[...], preferred_element_type=F32).astype(BF16)


def first_project(scaled, weights, late_values, groups, flag, weight, picks, tile):
    rows, width = scaled.shape
    columns = weight.shape[1] // lax.axis_size("head")
    steps = columns // tile
    whole = lambda x: pl.BlockSpec(x.shape, lambda g, t, f, k: (0, 0))
    return pl.pallas_call(
        functools.partial(first_project_kernel, groups, len(late_values)),
        out_shape=[
            jax.ShapeDtypeStruct((picks.shape[0] * rows, columns), BF16),
            jax.ShapeDtypeStruct((rows, width), BF16),
        ],
        grid_spec=pltpu.PrefetchScalarGridSpec(
            num_scalar_prefetch=2,
            grid=(picks.shape[0], steps),
            in_specs=[whole(scaled), whole(weights)]
            + [whole(v) for v in late_values]
            + [pl.BlockSpec((width, tile), lambda g, t, f, k: (0, k[g] * steps + t))],
            out_specs=[
                pl.BlockSpec((rows, tile), lambda g, t, f, k: (g, t)),
                pl.BlockSpec((rows, width), lambda g, t, f, k: (0, 0)),
            ],
        ),
        compiler_params=params(),
        cost_estimate=pl.CostEstimate(
            flops=2 * rows * width * columns * picks.shape[0],
            bytes_accessed=2 * width * columns * picks.shape[0],
            transcendentals=0,
        ),
        name="first_project",
    )(flag, picks, scaled, weights, *late_values, weight)


def project_kernel(pick_ref, a_ref, w_ref, out_ref):
    out_ref[...] = jnp.dot(a_ref[...], w_ref[...], preferred_element_type=F32).astype(BF16)


def project(attended, weight, picks, tile):
    rows, width = attended.shape
    columns = weight.shape[1] // lax.axis_size("head")
    steps = columns // tile
    return pl.pallas_call(
        project_kernel,
        out_shape=jax.ShapeDtypeStruct((picks.shape[0] * rows, columns), BF16),
        grid_spec=pltpu.PrefetchScalarGridSpec(
            num_scalar_prefetch=1,
            grid=(picks.shape[0], steps),
            in_specs=[
                pl.BlockSpec((rows, width), lambda g, t, k: (0, 0)),
                pl.BlockSpec((width, tile), lambda g, t, k: (0, k[g] * steps + t)),
            ],
            out_specs=pl.BlockSpec((rows, tile), lambda g, t, k: (g, t)),
        ),
        compiler_params=params(),
        cost_estimate=pl.CostEstimate(
            flops=2 * rows * width * columns * picks.shape[0],
            bytes_accessed=2 * width * columns * picks.shape[0],
            transcendentals=0,
        ),
        name="project",
    )(picks, attended, weight)


def on_device(queries, key_vectors, value_vectors, live_blocks, out_weight):
    frames = lax.axis_size("frame")
    own = lax.axis_index("frame")
    group = lax.axis_index("head")
    rows = queries.shape[0]

    early, late, groups, flag = plan(own, frames)
    flag = flag[None]
    early_bias = bias_of(early[1:], live_blocks, frames, rows)
    late_bias = bias_of(late, live_blocks, frames, rows)

    early_keys = early_hops(key_vectors, frames)
    early_values = early_hops(value_vectors, frames)
    late_keys = late_hops(key_vectors, early_keys, own, frames)
    late_values = late_hops(value_vectors, early_values, own, frames)

    sums, peaks, totals = early_attention(
        queries, key_vectors, value_vectors, early_bias, early_keys, early_values
    )
    weights, scaled = late_weights(
        queries, late_bias, sums, peaks, totals, late_keys, groups, flag
    )

    swap = lambda x, bit: send(x, "head", [(g, g ^ bit) for g in range(4)])
    tile = out_weight.shape[1] // 8
    away, attended = first_project(
        scaled, weights, late_values, groups, flag, out_weight,
        jnp.stack([group ^ 3, group ^ 2]), tile,
    )
    near = project(attended, out_weight, jnp.stack([group ^ 1, group]), tile)
    crossed = (away[rows:].astype(F32) + swap(away[:rows], 1).astype(F32)).astype(BF16)
    from_far = swap(crossed, 2)
    from_near = swap(near[:rows], 1)
    total = near[rows:].astype(F32) + from_near.astype(F32) + from_far.astype(F32)
    return total.astype(BF16)


def solution(mesh):
    placed = (
        P("frame", "head"),
        P("frame", "head"),
        P("frame", "head"),
        P("frame", None),
        P("head", None),
    )
    return jax.shard_map(
        on_device, mesh=mesh, in_specs=placed, out_specs=P("frame", "head"), check_vma=False
    )
```

```python
import functools
import math

import jax
import jax.numpy as jnp
from jax import lax
from jax.experimental import pallas as pl
from jax.experimental.pallas import tpu as pltpu
from jax.sharding import PartitionSpec as P

HDIM = 128
BLK = 64
EXP_SCALE = math.log2(math.e) / math.sqrt(HDIM)
DEAD = -1e30
F32 = jnp.float32
BF16 = jnp.bfloat16


def offsets_for(frames):
    result = [0]
    step = 1
    while step <= frames // 2:
        result.append(step)
        result.append(-step)
        step = step * 2
    return result


def send(x, axis, pairs):
    return lax.ppermute(x, axis, pairs)


def from_offset(x, frames, offset):
    return send(
        x, "frame", [(i + offset, i) for i in range(frames) if 0 <= i + offset < frames]
    )


def early_hops(x, frames):
    if frames != 8:
        return [from_offset(x, frames, o) for o in offsets_for(frames)[1:-2]]
    return [
        send(x, "frame", [(i, i ^ 2) for i in range(frames)]),
        send(x, "frame", [(i, i ^ 6) for i in (2, 3, 4, 5)]),
        send(x, "frame", [(i, i ^ 1) for i in range(frames)]),
    ]


def late_hops(x, hops, own, frames, hold):
    if frames != 8:
        return [from_offset(x, frames, o) for o in offsets_for(frames)[-2:]]
    outer, inner, _ = hops
    across = jnp.where((own == 2) | (own == 5), inner, outer)
    return [
        send(outer, "frame", [(i, i ^ 6) for i in (2, 3, 4, 5)]),
        send(inner, "frame", [(i, i ^ 2) for i in (2, 3, 4, 5)]),
        send(hold(across), "frame", [(i, i ^ 1) for i in (0, 2, 3, 4, 5, 7)]),
    ]


def plan(own, frames):
    if frames != 8:
        held = [own + o for o in offsets_for(frames)]
        return held[:-2], held[-2:], ((0,), (1,)), own >= 0
    middle = (own >= 2) & (own <= 5)
    odd = lax.rem(own, 2)
    flip = 1 - 2 * odd
    low = lax.rem(lax.div(own, 2), 2)
    outer = own + 2 - 4 * low
    early = [own, outer, jnp.where(middle, own - 2 + 4 * low, -1), own + flip]
    late = [jnp.where(own >= 4, own - 4, own + 4), own - flip]
    return early, late, ((0, 1), (2,)), middle


def params():
    return pltpu.CompilerParams(vmem_limit_bytes=20 << 20)


VMEM = pl.BlockSpec(memory_space=pltpu.VMEM)
SMEM = pl.BlockSpec(memory_space=pltpu.SMEM)


def fill_bias(bias_ref, live_ref, held, frames):
    blocks = live_ref.shape[0]
    left = lax.broadcasted_iota(jnp.int32, (8, 2 * BLK), 1) < BLK
    for n, frame in enumerate(held):
        inside = (frame >= 0) & (frame < frames)
        base = jnp.where(inside, frame, 0) * blocks
        for b in range(blocks):
            for c in range(0, blocks, 2):
                one, two = (
                    jnp.where(inside & (live_ref[b, base + c + d] > 0), 0.0, DEAD).astype(F32)
                    for d in (0, 1)
                )
                at = n * blocks * BLK + c * BLK
                bias_ref[8 * b : 8 * b + 8, at : at + 2 * BLK] = jnp.where(left, one, two)


def scores_of(q, key, bias_ref, n):
    rows = q.shape[0]
    s = lax.dot_general(q, key, (((1,), (1,)), ((), ())), preferred_element_type=F32)
    if bias_ref is None:
        return s
    parts = []
    for b in range(rows // BLK):
        bias = bias_ref[8 * b : 8 * b + 8, n * rows : (n + 1) * rows]
        part = s[b * BLK : (b + 1) * BLK].reshape(BLK // 8, 8, rows) + bias[None]
        parts.append(part.reshape(BLK, rows))
    return jnp.concatenate(parts, 0)


def each_head(heads, body, unroll):
    def some(step, _):
        for n in range(unroll):
            h = step * unroll + n
            body(h, pl.ds(pl.multiple_of(h * HDIM, HDIM), HDIM))
        return 0

    lax.fori_loop(0, heads // unroll, some, 0)


def early_kernel(count, live_ref, q_ref, k_ref, v_ref, *rest):
    keys, values = (k_ref, *rest[:count]), (v_ref, *rest[count : 2 * count])
    sum_ref, peak_ref, total_ref, bias_ref = rest[2 * count :]
    frames = lax.axis_size("frame")
    held = plan(lax.axis_index("frame"), frames)[0]
    fill_bias(bias_ref, live_ref, held[1:], frames)

    def head(h, columns):
        q = q_ref[:, columns]
        scores = []
        for n, ref in enumerate(keys):
            scores.append(scores_of(q, ref[:, columns], bias_ref if n else None, n - 1))
        peak = jnp.max(functools.reduce(jnp.maximum, scores), axis=1, keepdims=True)
        acc = None
        total = None
        for s, ref in zip(scores, values):
            e = jnp.exp2((s - peak) * EXP_SCALE)
            total = e if total is None else total + e
            part = jnp.dot(e.astype(BF16), ref[:, columns], preferred_element_type=F32)
            acc = part if acc is None else acc + part
        sum_ref[:, columns] = acc
        peak_ref[:, columns] = jnp.broadcast_to(peak, acc.shape)
        total_ref[:, columns] = jnp.broadcast_to(
            jnp.sum(total, axis=1, keepdims=True), acc.shape
        )

    each_head(q_ref.shape[1] // HDIM, head, 2)


def early_attention(live_blocks, queries, keys, values, early_keys, early_values):
    rows, width = queries.shape
    count = len(early_keys)
    seen = rows * (count + 1)
    heads = width // HDIM
    return pl.pallas_call(
        functools.partial(early_kernel, count),
        out_shape=[jax.ShapeDtypeStruct((rows, width), F32)] * 3,
        in_specs=[SMEM] + [VMEM] * (3 + 2 * count),
        out_specs=[VMEM] * 3,
        scratch_shapes=[pltpu.VMEM((8 * rows // BLK, count * rows), F32)],
        compiler_params=params(),
        cost_estimate=pl.CostEstimate(
            flops=4 * heads * rows * seen * HDIM,
            bytes_accessed=4 * heads * seen * HDIM,
            transcendentals=heads * rows * seen,
        ),
        name="early_attention",
    )(live_blocks, queries, keys, values, *early_keys, *early_values)


def pick(refs, group, columns, first):
    if len(group) == 1:
        return refs[group[0]][:, columns]
    one, two = (refs[g][:, columns] for g in group)
    return jnp.where(first, one, two)


def late_kernel(live_ref, q_ref, sum_ref, peak_ref, total_ref, *rest):
    keys, (weight_ref, scaled_ref, bias_ref) = rest[:-3], rest[-3:]
    frames = lax.axis_size("frame")
    _, held, groups, first = plan(lax.axis_index("frame"), frames)
    rows = q_ref.shape[0]
    seen = rows * len(groups)
    fill_bias(bias_ref, live_ref, held, frames)

    def head(h, columns):
        q = q_ref[:, columns]
        scores = [
            scores_of(q, pick(keys, group, columns, first), bias_ref, n)
            for n, group in enumerate(groups)
        ]
        before = peak_ref[:, columns]
        peak = jnp.max(functools.reduce(jnp.maximum, scores), axis=1, keepdims=True)
        peak = jnp.maximum(before, jnp.broadcast_to(peak, before.shape))
        expos = []
        for s in scores:
            for c in range(0, rows, HDIM):
                expos.append(jnp.exp2((s[:, c : c + HDIM] - peak) * EXP_SCALE))
        total = jnp.sum(functools.reduce(jnp.add, expos), axis=1, keepdims=True)
        shrink = jnp.exp2((before - peak) * EXP_SCALE)
        over = 1.0 / (total_ref[:, columns] * shrink + jnp.broadcast_to(total, before.shape))
        for n, e in enumerate(expos):
            at = pl.multiple_of(h * seen + n * HDIM, HDIM)
            weight_ref[:, pl.ds(at, HDIM)] = (e * over).astype(BF16)
        scaled_ref[:, columns] = sum_ref[:, columns] * (shrink * over)

    each_head(q_ref.shape[1] // HDIM, head, 2)


def late_weights(live_blocks, queries, sums, peaks, totals, late_keys, places):
    rows, width = queries.shape
    heads = width // HDIM
    seen = rows * places
    return pl.pallas_call(
        late_kernel,
        out_shape=[
            jax.ShapeDtypeStruct((rows, heads * seen), BF16),
            jax.ShapeDtypeStruct((rows, width), F32),
        ],
        in_specs=[SMEM] + [VMEM] * (4 + len(late_keys)),
        out_specs=[VMEM] * 2,
        scratch_shapes=[pltpu.VMEM((8 * rows // BLK, seen), F32)],
        compiler_params=params(),
        cost_estimate=pl.CostEstimate(
            flops=2 * heads * rows * seen * HDIM,
            bytes_accessed=4 * heads * seen * HDIM,
            transcendentals=heads * rows * seen,
        ),
        name="late_weights",
    )(live_blocks, queries, sums, peaks, totals, *late_keys)


def multiply(a_ref, w_ref, out_ref, group):
    width = out_ref.shape[1]
    step = width // 5 if width % (5 * HDIM) == 0 else width
    for n in range(0, width, step):
        columns = pl.ds(pl.multiple_of(group * width + n, HDIM), step)
        out_ref[:, n : n + step] = jnp.dot(
            a_ref[...], w_ref[:, columns], preferred_element_type=F32
        ).astype(BF16)


def first_project_kernel(count, scaled_ref, weights_ref, *rest):
    values = rest[:count]
    w_ref, out_ref, att_ref = rest[count:]
    rows, width = scaled_ref.shape
    _, _, groups, first = plan(lax.axis_index("frame"), lax.axis_size("frame"))
    seen = rows * len(groups)
    for h in range(width // HDIM):
        columns = slice(h * HDIM, (h + 1) * HDIM)
        acc = scaled_ref[:, columns]
        for n, group in enumerate(groups):
            value = pick(values, group, columns, first)
            weight = weights_ref[:, h * seen + n * rows : h * seen + (n + 1) * rows]
            acc += jnp.dot(weight, value, preferred_element_type=F32)
        att_ref[:, columns] = acc.astype(BF16)
    multiply(att_ref, w_ref, out_ref, lax.axis_index("head") ^ 3)


def project_cost(rows, width, columns, count):
    return pl.CostEstimate(
        flops=2 * rows * width * columns * count,
        bytes_accessed=2 * width * columns * count,
        transcendentals=0,
    )


def first_project(scaled, weights, late_values, weight):
    rows, width = scaled.shape
    columns = weight.shape[1] // lax.axis_size("head")
    return pl.pallas_call(
        functools.partial(first_project_kernel, len(late_values)),
        out_shape=[
            jax.ShapeDtypeStruct((rows, columns), BF16),
            jax.ShapeDtypeStruct((rows, width), BF16),
        ],
        in_specs=[VMEM] * (3 + len(late_values)),
        out_specs=[VMEM] * 2,
        compiler_params=params(),
        cost_estimate=project_cost(rows, width, columns, 1),
        name="first_project",
    )(scaled, weights, *late_values, weight)


def project_kernel(bits, a_ref, w_ref, *outs):
    for bit, out_ref in zip(bits, outs):
        multiply(a_ref, w_ref, out_ref, lax.axis_index("head") ^ bit)


def project(attended, weight, bits):
    rows, width = attended.shape
    columns = weight.shape[1] // lax.axis_size("head")
    return pl.pallas_call(
        functools.partial(project_kernel, bits),
        out_shape=[jax.ShapeDtypeStruct((rows, columns), BF16)] * len(bits),
        in_specs=[VMEM] * 2,
        out_specs=[VMEM] * len(bits),
        compiler_params=params(),
        cost_estimate=project_cost(rows, width, columns, len(bits)),
        name="project",
    )(attended, weight)


def after(x, *others):
    return lax.optimization_barrier((x, *others))[0]


def on_device(queries, key_vectors, value_vectors, live_blocks, out_weight):
    frames = lax.axis_size("frame")
    own = lax.axis_index("frame")

    early_keys = early_hops(key_vectors, frames)
    early_values = early_hops(value_vectors, frames)
    late_keys = late_hops(key_vectors, early_keys, own, frames, lambda x: after(x, early_values[0]))

    sums, peaks, totals = early_attention(
        live_blocks, queries, key_vectors, value_vectors, early_keys, early_values
    )
    late_values = late_hops(value_vectors, early_values, own, frames, lambda x: after(x, sums))
    places = 2
    weights, scaled = late_weights(
        live_blocks, queries, sums, peaks, totals, late_keys, places
    )

    swap = lambda x, bit: send(x, "head", [(g, g ^ bit) for g in range(4)])
    for_sibling, attended = first_project(scaled, weights, late_values, out_weight)
    (mine,) = project(attended, out_weight, (2,))
    crossed = (mine.astype(F32) + swap(for_sibling, 1).astype(F32)).astype(BF16)
    from_far = swap(crossed, 2)
    near, total = project(after(attended, crossed), out_weight, (1, 0))
    from_near = swap(near, 1)
    total = total.astype(F32) + from_near.astype(F32) + from_far.astype(F32)
    return total.astype(BF16)


def solution(mesh):
    placed = (
        P("frame", "head"),
        P("frame", "head"),
        P("frame", "head"),
        P("frame", None),
        P("head", None),
    )
    return jax.shard_map(
        on_device, mesh=mesh, in_specs=placed, out_specs=P("frame", "head"), check_vma=False
    )
```

```python
import functools
import math

import jax
import jax.numpy as jnp
from jax import lax
from jax.experimental import pallas as pl
from jax.experimental.pallas import tpu as pltpu
from jax.sharding import PartitionSpec as P

HDIM = 128
BLK = 64
EXP_SCALE = math.log2(math.e) / math.sqrt(HDIM)
DEAD = -1e30
BARS = {'XV': ('E2K',), 'F1K': ('E1K',), 'DK': ('XK', 'E1K'), 'F1V': ('S', 'F2K'), 'F2V': ('XV',)}
F32 = jnp.float32
BF16 = jnp.bfloat16
LIGHT = pl.CostEstimate(flops=0, bytes_accessed=0, transcendentals=0)


def offsets_for(frames):
    result = [0]
    step = 1
    while step <= frames // 2:
        result.append(step)
        result.append(-step)
        step = step * 2
    return result


def send(x, axis, pairs):
    return lax.ppermute(x, axis, pairs)


def from_offset(x, frames, offset):
    return send(
        x, "frame", [(i + offset, i) for i in range(frames) if 0 <= i + offset < frames]
    )


def wait(x, name, done):
    return after(x, *(done[n] for n in BARS.get(name, ())))


def early_hops(x, frames, kind, done):
    if frames != 8:
        return [from_offset(x, frames, o) for o in offsets_for(frames)[1:-2]]
    hops = []
    for name, pairs in (
        ("E1", [(i, i ^ 2) for i in range(frames)]),
        ("E2", [(i, i ^ 6) for i in (2, 3, 4, 5)]),
        ("X", [(i, i ^ 1) for i in range(frames)]),
    ):
        hops.append(send(wait(x, name + kind, done), "frame", pairs))
        done[name + kind] = hops[-1]
    return hops


def late_hops(x, hops, own, frames, kind, done):
    if frames != 8:
        return [from_offset(x, frames, o) for o in offsets_for(frames)[-2:]]
    outer, inner, _ = hops
    across = jnp.where((own == 2) | (own == 5), inner, outer)
    results = []
    for name, x, pairs in (
        ("F1", outer, [(i, i ^ 6) for i in (2, 3, 4, 5)]),
        ("F2", inner, [(i, i ^ 2) for i in (2, 3, 4, 5)]),
        ("D", across, [(i, i ^ 1) for i in (0, 2, 3, 4, 5, 7)]),
    ):
        results.append(send(wait(x, name + kind, done), "frame", pairs))
        done[name + kind] = results[-1]
    return results


def plan(own, frames):
    if frames != 8:
        held = [own + o for o in offsets_for(frames)]
        return held[:-2], held[-2:], ((0,), (1,)), own >= 0
    middle = (own >= 2) & (own <= 5)
    odd = lax.rem(own, 2)
    flip = 1 - 2 * odd
    low = lax.rem(lax.div(own, 2), 2)
    outer = own + 2 - 4 * low
    early = [own, outer, jnp.where(middle, own - 2 + 4 * low, -1), own + flip]
    late = [jnp.where(own >= 4, own - 4, own + 4), own - flip]
    return early, late, ((0, 1), (2,)), middle


def params():
    return pltpu.CompilerParams(vmem_limit_bytes=20 << 20)


VMEM = pl.BlockSpec(memory_space=pltpu.VMEM)
SMEM = pl.BlockSpec(memory_space=pltpu.SMEM)


def fill_bias(bias_ref, live_ref, held, frames):
    blocks = live_ref.shape[0]
    left = lax.broadcasted_iota(jnp.int32, (8, 2 * BLK), 1) < BLK
    for n, frame in enumerate(held):
        inside = (frame >= 0) & (frame < frames)
        base = jnp.where(inside, frame, 0) * blocks
        for b in range(blocks):
            for c in range(0, blocks, 2):
                one, two = (
                    jnp.where(inside & (live_ref[b, base + c + d] > 0), 0.0, DEAD).astype(F32)
                    for d in (0, 1)
                )
                at = n * blocks * BLK + c * BLK
                bias_ref[8 * b : 8 * b + 8, at : at + 2 * BLK] = jnp.where(left, one, two)


def scores_of(q, key, bias_ref, n):
    rows = q.shape[0]
    s = lax.dot_general(q, key, (((1,), (1,)), ((), ())), preferred_element_type=F32)
    if bias_ref is None:
        return s
    parts = []
    for b in range(rows // BLK):
        bias = bias_ref[8 * b : 8 * b + 8, n * rows : (n + 1) * rows]
        part = s[b * BLK : (b + 1) * BLK].reshape(BLK // 8, 8, rows) + bias[None]
        parts.append(part.reshape(BLK, rows))
    return jnp.concatenate(parts, 0)


def each_head(heads, body, unroll):
    def some(step, _):
        for n in range(unroll):
            h = step * unroll + n
            body(h, pl.ds(pl.multiple_of(h * HDIM, HDIM), HDIM))
        return 0

    lax.fori_loop(0, heads // unroll, some, 0)


def early_kernel(count, live_ref, q_ref, k_ref, v_ref, *rest):
    keys, values = (k_ref, *rest[:count]), (v_ref, *rest[count : 2 * count])
    sum_ref, peak_ref, total_ref, bias_ref = rest[2 * count :]
    frames = lax.axis_size("frame")
    held = plan(lax.axis_index("frame"), frames)[0]
    fill_bias(bias_ref, live_ref, held[1:], frames)

    def head(h, columns):
        q = q_ref[:, columns]
        scores = []
        for n, ref in enumerate(keys):
            scores.append(scores_of(q, ref[:, columns], bias_ref if n else None, n - 1))
        peak = jnp.max(functools.reduce(jnp.maximum, scores), axis=1, keepdims=True)
        acc = None
        total = None
        for s, ref in zip(scores, values):
            e = jnp.exp2((s - peak) * EXP_SCALE)
            total = e if total is None else total + e
            part = jnp.dot(e.astype(BF16), ref[:, columns], preferred_element_type=F32)
            acc = part if acc is None else acc + part
        sum_ref[:, columns] = acc
        peak_ref[:, columns] = jnp.broadcast_to(peak, acc.shape)
        total_ref[:, columns] = jnp.broadcast_to(
            jnp.sum(total, axis=1, keepdims=True), acc.shape
        )

    each_head(q_ref.shape[1] // HDIM, head, 2)


def early_attention(live_blocks, queries, keys, values, early_keys, early_values):
    rows, width = queries.shape
    count = len(early_keys)
    seen = rows * (count + 1)
    heads = width // HDIM
    return pl.pallas_call(
        functools.partial(early_kernel, count),
        out_shape=[jax.ShapeDtypeStruct((rows, width), F32)] * 3,
        in_specs=[SMEM] + [VMEM] * (3 + 2 * count),
        out_specs=[VMEM] * 3,
        scratch_shapes=[pltpu.VMEM((8 * rows // BLK, count * rows), F32)],
        compiler_params=params(),
        cost_estimate=LIGHT,
        name="early_attention",
    )(live_blocks, queries, keys, values, *early_keys, *early_values)


def pick(refs, group, columns, first):
    if len(group) == 1:
        return refs[group[0]][:, columns]
    one, two = (refs[g][:, columns] for g in group)
    return jnp.where(first, one, two)


def late_kernel(live_ref, q_ref, sum_ref, peak_ref, total_ref, *rest):
    keys, (weight_ref, scaled_ref, bias_ref) = rest[:-3], rest[-3:]
    frames = lax.axis_size("frame")
    _, held, groups, first = plan(lax.axis_index("frame"), frames)
    rows = q_ref.shape[0]
    seen = rows * len(groups)
    fill_bias(bias_ref, live_ref, held, frames)

    def head(h, columns):
        q = q_ref[:, columns]
        scores = [
            scores_of(q, pick(keys, group, columns, first), bias_ref, n)
            for n, group in enumerate(groups)
        ]
        before = peak_ref[:, columns]
        peak = jnp.max(functools.reduce(jnp.maximum, scores), axis=1, keepdims=True)
        peak = jnp.maximum(before, jnp.broadcast_to(peak, before.shape))
        expos = []
        for s in scores:
            for c in range(0, rows, HDIM):
                expos.append(jnp.exp2((s[:, c : c + HDIM] - peak) * EXP_SCALE))
        total = jnp.sum(functools.reduce(jnp.add, expos), axis=1, keepdims=True)
        shrink = jnp.exp2((before - peak) * EXP_SCALE)
        over = 1.0 / (total_ref[:, columns] * shrink + jnp.broadcast_to(total, before.shape))
        for n, e in enumerate(expos):
            at = pl.multiple_of(h * seen + n * HDIM, HDIM)
            weight_ref[:, pl.ds(at, HDIM)] = (e * over).astype(BF16)
        scaled_ref[:, columns] = sum_ref[:, columns] * (shrink * over)

    each_head(q_ref.shape[1] // HDIM, head, 2)


def late_weights(live_blocks, queries, sums, peaks, totals, late_keys, places):
    rows, width = queries.shape
    heads = width // HDIM
    seen = rows * places
    return pl.pallas_call(
        late_kernel,
        out_shape=[
            jax.ShapeDtypeStruct((rows, heads * seen), BF16),
            jax.ShapeDtypeStruct((rows, width), F32),
        ],
        in_specs=[SMEM] + [VMEM] * (4 + len(late_keys)),
        out_specs=[VMEM] * 2,
        scratch_shapes=[pltpu.VMEM((8 * rows // BLK, seen), F32)],
        compiler_params=params(),
        cost_estimate=LIGHT,
        name="late_weights",
    )(live_blocks, queries, sums, peaks, totals, *late_keys)


def multiply(a_ref, w_ref, out_ref, *parts):
    columns = w_ref.shape[1] // lax.axis_size("head")
    step = 2 * HDIM
    base = 0
    for bit, start, width in parts:
        group = lax.axis_index("head") ^ bit
        for n in range(0, width, step):
            at = pl.ds(pl.multiple_of(group * columns + (start + n), HDIM), step)
            out_ref[:, base + n : base + n + step] = jnp.dot(
                a_ref[...], w_ref[:, at], preferred_element_type=F32
            ).astype(BF16)
        base += width


def first_project_kernel(count, scaled_ref, weights_ref, *rest):
    values = rest[:count]
    w_ref, out_ref, att_ref = rest[count:]
    rows, width = scaled_ref.shape
    _, _, groups, first = plan(lax.axis_index("frame"), lax.axis_size("frame"))
    seen = rows * len(groups)
    for h in range(width // HDIM):
        columns = slice(h * HDIM, (h + 1) * HDIM)
        acc = scaled_ref[:, columns]
        for n, group in enumerate(groups):
            value = pick(values, group, columns, first)
            weight = weights_ref[:, h * seen + n * rows : h * seen + (n + 1) * rows]
            acc += jnp.dot(weight, value, preferred_element_type=F32)
        att_ref[:, columns] = acc.astype(BF16)
    multiply(att_ref, w_ref, out_ref, (3, 0, out_ref.shape[1]))


def first_project(scaled, weights, late_values, weight, columns):
    rows, width = scaled.shape
    return pl.pallas_call(
        functools.partial(first_project_kernel, len(late_values)),
        out_shape=[
            jax.ShapeDtypeStruct((rows, columns), BF16),
            jax.ShapeDtypeStruct((rows, width), BF16),
        ],
        in_specs=[VMEM] * (3 + len(late_values)),
        out_specs=[VMEM] * 2,
        compiler_params=params(),
        cost_estimate=LIGHT,
        name="first_project",
    )(scaled, weights, *late_values, weight)


def project_kernel(outputs, a_ref, w_ref, *outs):
    for parts, out_ref in zip(outputs, outs):
        multiply(a_ref, w_ref, out_ref, *parts)


def project(attended, weight, *outputs):
    rows = attended.shape[0]
    return pl.pallas_call(
        functools.partial(project_kernel, outputs),
        out_shape=[
            jax.ShapeDtypeStruct((rows, sum(width for _, _, width in parts)), BF16)
            for parts in outputs
        ],
        in_specs=[VMEM] * 2,
        out_specs=[VMEM] * len(outputs),
        compiler_params=params(),
        cost_estimate=LIGHT,
        name="project",
    )(attended, weight)


def after(x, *others):
    return lax.optimization_barrier((x, *others))[0] if others else x


def on_device(queries, key_vectors, value_vectors, live_blocks, out_weight):
    frames = lax.axis_size("frame")
    own = lax.axis_index("frame")

    done = {}
    early_keys = early_hops(key_vectors, frames, "K", done)
    early_values = early_hops(value_vectors, frames, "V", done)
    late_keys = late_hops(key_vectors, early_keys, own, frames, "K", done)
    held_queries = wait(queries, "S", done) if frames == 8 else queries
    sums, peaks, totals = early_attention(
        live_blocks, held_queries, key_vectors, value_vectors, early_keys, early_values
    )
    done["S"] = sums
    late_values = late_hops(value_vectors, early_values, own, frames, "V", done)
    places = 2
    weights, scaled = late_weights(
        live_blocks, queries, sums, peaks, totals, late_keys, places
    )

    swap = lambda x, bit: send(x, "head", [(g, g ^ bit) for g in range(4)])
    add = lambda a, b: (a.astype(F32) + b.astype(F32)).astype(BF16)
    columns = out_weight.shape[1] // lax.axis_size("head")
    for_sibling, attended = first_project(scaled, weights, late_values, out_weight, columns)
    (mine,) = project(attended, out_weight, ((2, 0, columns),))
    crossed = add(mine, swap(for_sibling, 1))
    near_a, near_b, total = project(after(attended, crossed), out_weight, ((1, 0, columns // 5 * 2),), ((1, columns // 5 * 2, columns // 5 * 3),), ((0, 0, columns),))
    from_near = jnp.concatenate([swap(near_a, 1), swap(near_b, 1)], 1)
    from_far = swap(crossed, 2)
    total = total.astype(F32) + from_near.astype(F32) + from_far.astype(F32)
    return total.astype(BF16)


def solution(mesh):
    placed = (
        P("frame", "head"),
        P("frame", "head"),
        P("frame", "head"),
        P("frame", None),
        P("head", None),
    )
    return jax.shard_map(
        on_device, mesh=mesh, in_specs=placed, out_specs=P("frame", "head"), check_vma=False
    )
```

```python
import functools
import math

import jax
import jax.numpy as jnp
from jax import lax
from jax.experimental import pallas as pl
from jax.experimental.pallas import tpu as pltpu
from jax.sharding import PartitionSpec as P

HDIM = 128
BLK = 64
EXP_SCALE = math.log2(math.e) / math.sqrt(HDIM)
DEAD = -1e30
BARS = {'XV': ('E1K', 'XK'), 'F1K': ('E2K', 'E1V'), 'F1V': ('S',), 'DV': ('XV',)}
F32 = jnp.float32
BF16 = jnp.bfloat16
LIGHT = pl.CostEstimate(flops=0, bytes_accessed=0, transcendentals=0)


def offsets_for(frames):
    result = [0]
    step = 1
    while step <= frames // 2:
        result.append(step)
        result.append(-step)
        step = step * 2
    return result


def send(x, axis, pairs):
    return lax.ppermute(x, axis, pairs)


def from_offset(x, frames, offset):
    return send(
        x, "frame", [(i + offset, i) for i in range(frames) if 0 <= i + offset < frames]
    )


def wait(x, name, done):
    return after(x, *(done[n] for n in BARS.get(name, ())))


def early_hops(x, frames, kind, done):
    if frames != 8:
        return [from_offset(x, frames, o) for o in offsets_for(frames)[1:-2]]
    hops = []
    for name, pairs in (
        ("E1", [(i, i ^ 2) for i in range(frames)]),
        ("E2", [(i, i ^ 6) for i in (2, 3, 4, 5)]),
        ("X", [(i, i ^ 1) for i in range(frames)]),
    ):
        hops.append(send(wait(x, name + kind, done), "frame", pairs))
        done[name + kind] = hops[-1]
    return hops


def late_hops(x, hops, own, frames, kind, done):
    if frames != 8:
        return [from_offset(x, frames, o) for o in offsets_for(frames)[-2:]]
    outer, inner, _ = hops
    across = jnp.where((own == 2) | (own == 5), inner, outer)
    results = []
    for name, x, pairs in (
        ("F1", outer, [(i, i ^ 6) for i in (2, 3, 4, 5)]),
        ("F2", inner, [(i, i ^ 2) for i in (2, 3, 4, 5)]),
        ("D", across, [(i, i ^ 1) for i in (0, 2, 3, 4, 5, 7)]),
    ):
        results.append(send(wait(x, name + kind, done), "frame", pairs))
        done[name + kind] = results[-1]
    return results


def plan(own, frames):
    if frames != 8:
        held = [own + o for o in offsets_for(frames)]
        return held[:-2], held[-2:], ((0,), (1,)), own >= 0
    middle = (own >= 2) & (own <= 5)
    odd = lax.rem(own, 2)
    flip = 1 - 2 * odd
    low = lax.rem(lax.div(own, 2), 2)
    outer = own + 2 - 4 * low
    early = [own, outer, jnp.where(middle, own - 2 + 4 * low, -1), own + flip]
    late = [jnp.where(own >= 4, own - 4, own + 4), own - flip]
    return early, late, ((0, 1), (2,)), middle


def params():
    return pltpu.CompilerParams(vmem_limit_bytes=20 << 20)


VMEM = pl.BlockSpec(memory_space=pltpu.VMEM)
SMEM = pl.BlockSpec(memory_space=pltpu.SMEM)


def fill_bias(bias_ref, live_ref, held, frames):
    blocks = live_ref.shape[0]
    left = lax.broadcasted_iota(jnp.int32, (8, 2 * BLK), 1) < BLK
    for n, frame in enumerate(held):
        inside = (frame >= 0) & (frame < frames)
        base = jnp.where(inside, frame, 0) * blocks
        for b in range(blocks):
            for c in range(0, blocks, 2):
                one, two = (
                    jnp.where(inside & (live_ref[b, base + c + d] > 0), 0.0, DEAD).astype(F32)
                    for d in (0, 1)
                )
                at = n * blocks * BLK + c * BLK
                bias_ref[8 * b : 8 * b + 8, at : at + 2 * BLK] = jnp.where(left, one, two)


def scores_of(q, key, bias_ref, n):
    rows = q.shape[0]
    s = lax.dot_general(q, key, (((1,), (1,)), ((), ())), preferred_element_type=F32)
    if bias_ref is None:
        return s
    parts = []
    for b in range(rows // BLK):
        bias = bias_ref[8 * b : 8 * b + 8, n * rows : (n + 1) * rows]
        part = s[b * BLK : (b + 1) * BLK].reshape(BLK // 8, 8, rows) + bias[None]
        parts.append(part.reshape(BLK, rows))
    return jnp.concatenate(parts, 0)


def each_head(heads, body, unroll):
    def some(step, _):
        for n in range(unroll):
            h = step * unroll + n
            body(h, pl.ds(pl.multiple_of(h * HDIM, HDIM), HDIM))
        return 0

    lax.fori_loop(0, heads // unroll, some, 0)


def early_kernel(count, live_ref, q_ref, k_ref, v_ref, *rest):
    keys, values = (k_ref, *rest[:count]), (v_ref, *rest[count : 2 * count])
    sum_ref, peak_ref, total_ref, bias_ref = rest[2 * count :]
    frames = lax.axis_size("frame")
    held = plan(lax.axis_index("frame"), frames)[0]
    fill_bias(bias_ref, live_ref, held[1:], frames)

    def head(h, columns):
        q = q_ref[:, columns]
        scores = []
        for n, ref in enumerate(keys):
            scores.append(scores_of(q, ref[:, columns], bias_ref if n else None, n - 1))
        peak = jnp.max(functools.reduce(jnp.maximum, scores), axis=1, keepdims=True)
        acc = None
        total = None
        for s, ref in zip(scores, values):
            e = jnp.exp2((s - peak) * EXP_SCALE)
            total = e if total is None else total + e
            part = jnp.dot(e.astype(BF16), ref[:, columns], preferred_element_type=F32)
            acc = part if acc is None else acc + part
        sum_ref[:, columns] = acc
        peak_ref[:, columns] = jnp.broadcast_to(peak, acc.shape)
        total_ref[:, columns] = jnp.broadcast_to(
            jnp.sum(total, axis=1, keepdims=True), acc.shape
        )

    each_head(q_ref.shape[1] // HDIM, head, 2)


def early_attention(live_blocks, queries, keys, values, early_keys, early_values):
    rows, width = queries.shape
    count = len(early_keys)
    seen = rows * (count + 1)
    heads = width // HDIM
    return pl.pallas_call(
        functools.partial(early_kernel, count),
        out_shape=[jax.ShapeDtypeStruct((rows, width), F32)] * 3,
        in_specs=[SMEM] + [VMEM] * (3 + 2 * count),
        out_specs=[VMEM] * 3,
        scratch_shapes=[pltpu.VMEM((8 * rows // BLK, count * rows), F32)],
        compiler_params=params(),
        cost_estimate=LIGHT,
        name="early_attention",
    )(live_blocks, queries, keys, values, *early_keys, *early_values)


def pick(refs, group, columns, first):
    if len(group) == 1:
        return refs[group[0]][:, columns]
    one, two = (refs[g][:, columns] for g in group)
    return jnp.where(first, one, two)


def late_kernel(live_ref, q_ref, sum_ref, peak_ref, total_ref, *rest):
    keys, (weight_ref, scaled_ref, bias_ref) = rest[:-3], rest[-3:]
    frames = lax.axis_size("frame")
    _, held, groups, first = plan(lax.axis_index("frame"), frames)
    rows = q_ref.shape[0]
    seen = rows * len(groups)
    fill_bias(bias_ref, live_ref, held, frames)

    def head(h, columns):
        q = q_ref[:, columns]
        scores = [
            scores_of(q, pick(keys, group, columns, first), bias_ref, n)
            for n, group in enumerate(groups)
        ]
        before = peak_ref[:, columns]
        peak = jnp.max(functools.reduce(jnp.maximum, scores), axis=1, keepdims=True)
        peak = jnp.maximum(before, jnp.broadcast_to(peak, before.shape))
        expos = []
        for s in scores:
            for c in range(0, rows, HDIM):
                expos.append(jnp.exp2((s[:, c : c + HDIM] - peak) * EXP_SCALE))
        total = jnp.sum(functools.reduce(jnp.add, expos), axis=1, keepdims=True)
        shrink = jnp.exp2((before - peak) * EXP_SCALE)
        over = 1.0 / (total_ref[:, columns] * shrink + jnp.broadcast_to(total, before.shape))
        for n, e in enumerate(expos):
            at = pl.multiple_of(h * seen + n * HDIM, HDIM)
            weight_ref[:, pl.ds(at, HDIM)] = (e * over).astype(BF16)
        scaled_ref[:, columns] = sum_ref[:, columns] * (shrink * over)

    each_head(q_ref.shape[1] // HDIM, head, 2)


def late_weights(live_blocks, queries, sums, peaks, totals, late_keys, places):
    rows, width = queries.shape
    heads = width // HDIM
    seen = rows * places
    return pl.pallas_call(
        late_kernel,
        out_shape=[
            jax.ShapeDtypeStruct((rows, heads * seen), BF16),
            jax.ShapeDtypeStruct((rows, width), F32),
        ],
        in_specs=[SMEM] + [VMEM] * (4 + len(late_keys)),
        out_specs=[VMEM] * 2,
        scratch_shapes=[pltpu.VMEM((8 * rows // BLK, seen), F32)],
        compiler_params=params(),
        cost_estimate=LIGHT,
        name="late_weights",
    )(live_blocks, queries, sums, peaks, totals, *late_keys)


def multiply(a_ref, w_ref, out_ref, *parts):
    columns = w_ref.shape[1] // lax.axis_size("head")
    base = 0
    for bit, start, width in parts:
        group = lax.axis_index("head") ^ bit
        for n in range(0, width, 2 * HDIM):
            step = min(2 * HDIM, width - n)
            at = pl.ds(pl.multiple_of(group * columns + (start + n), HDIM), step)
            out_ref[:, base + n : base + n + step] = jnp.dot(
                a_ref[...], w_ref[:, at], preferred_element_type=F32
            ).astype(BF16)
        base += width


def first_project_kernel(count, scaled_ref, weights_ref, *rest):
    values = rest[:count]
    w_ref, out_ref, att_ref = rest[count:]
    rows, width = scaled_ref.shape
    _, _, groups, first = plan(lax.axis_index("frame"), lax.axis_size("frame"))
    seen = rows * len(groups)
    for h in range(width // HDIM):
        columns = slice(h * HDIM, (h + 1) * HDIM)
        acc = scaled_ref[:, columns]
        for n, group in enumerate(groups):
            value = pick(values, group, columns, first)
            weight = weights_ref[:, h * seen + n * rows : h * seen + (n + 1) * rows]
            acc += jnp.dot(weight, value, preferred_element_type=F32)
        att_ref[:, columns] = acc.astype(BF16)
    multiply(att_ref, w_ref, out_ref, (3, 0, out_ref.shape[1]))


def first_project(scaled, weights, late_values, weight, columns):
    rows, width = scaled.shape
    return pl.pallas_call(
        functools.partial(first_project_kernel, len(late_values)),
        out_shape=[
            jax.ShapeDtypeStruct((rows, columns), BF16),
            jax.ShapeDtypeStruct((rows, width), BF16),
        ],
        in_specs=[VMEM] * (3 + len(late_values)),
        out_specs=[VMEM] * 2,
        compiler_params=params(),
        cost_estimate=LIGHT,
        name="first_project",
    )(scaled, weights, *late_values, weight)


def project_kernel(outputs, a_ref, w_ref, *outs):
    for parts, out_ref in zip(outputs, outs):
        multiply(a_ref, w_ref, out_ref, *parts)


def project(attended, weight, *outputs):
    rows = attended.shape[0]
    return pl.pallas_call(
        functools.partial(project_kernel, outputs),
        out_shape=[
            jax.ShapeDtypeStruct((rows, sum(width for _, _, width in parts)), BF16)
            for parts in outputs
        ],
        in_specs=[VMEM] * 2,
        out_specs=[VMEM] * len(outputs),
        compiler_params=params(),
        cost_estimate=LIGHT,
        name="project",
    )(attended, weight)


def after(x, *others):
    return lax.optimization_barrier((x, *others))[0] if others else x


def on_device(queries, key_vectors, value_vectors, live_blocks, out_weight):
    frames = lax.axis_size("frame")
    own = lax.axis_index("frame")

    done = {}
    early_keys = early_hops(key_vectors, frames, "K", done)
    early_values = early_hops(value_vectors, frames, "V", done)
    late_keys = late_hops(key_vectors, early_keys, own, frames, "K", done)
    held_queries = wait(queries, "S", done) if frames == 8 else queries
    sums, peaks, totals = early_attention(
        live_blocks, held_queries, key_vectors, value_vectors, early_keys, early_values
    )
    done["S"] = sums
    late_values = late_hops(value_vectors, early_values, own, frames, "V", done)
    places = 2
    weights, scaled = late_weights(
        live_blocks, queries, sums, peaks, totals, late_keys, places
    )

    swap = lambda x, bit: send(x, "head", [(g, g ^ bit) for g in range(4)])
    add = lambda a, b: (a.astype(F32) + b.astype(F32)).astype(BF16)
    columns = out_weight.shape[1] // lax.axis_size("head")
    cut = columns // 2
    rest = columns - cut
    sibling_a, attended = first_project(scaled, weights, late_values, out_weight, cut)
    sibling_b, mine_a = project(attended, out_weight, ((3, cut, rest),), ((2, 0, cut),))
    crossed_a = add(mine_a, swap(sibling_a, 1))
    far_a = swap(crossed_a, 2)
    sibling_b = swap(after(sibling_b, crossed_a), 1)
    (mine_b,) = project(after(attended, crossed_a), out_weight, ((2, cut, rest),))
    crossed_b = add(mine_b, sibling_b)
    far_b = swap(crossed_b, 2)
    bounds = [0, 4 * HDIM, 8 * HDIM, columns]
    *near, total = project(
        after(attended, crossed_b), out_weight,
        *(((1, p, q - p),) for p, q in zip(bounds[:-1], bounds[1:])), ((0, 0, columns),),
    )
    near = jnp.concatenate([swap(part, 1) for part in near], 1)
    total = total.astype(F32) + near.astype(F32)
    far = jnp.concatenate([far_a, far_b], 1)
    return (total + far.astype(F32)).astype(BF16)


def solution(mesh):
    placed = (
        P("frame", "head"),
        P("frame", "head"),
        P("frame", "head"),
        P("frame", None),
        P("head", None),
    )
    return jax.shard_map(
        on_device, mesh=mesh, in_specs=placed, out_specs=P("frame", "head"), check_vma=False
    )
```

```python
import functools
import math

import jax
import jax.numpy as jnp
from jax import lax
from jax.experimental import pallas as pl
from jax.experimental.pallas import tpu as pltpu
from jax.sharding import PartitionSpec as P

HDIM = 128
BLK = 64
EXP_SCALE = math.log2(math.e) / math.sqrt(HDIM)
DEAD = -1e30
BARS = {'XV': ('E1K', 'XK'), 'F1K': ('E2K', 'E1V'), 'F1V': ('S',), 'DV': ('XV',)}
F32 = jnp.float32
BF16 = jnp.bfloat16
LIGHT = pl.CostEstimate(flops=0, bytes_accessed=0, transcendentals=0)


def offsets_for(frames):
    result = [0]
    step = 1
    while step <= frames // 2:
        result.append(step)
        result.append(-step)
        step = step * 2
    return result


def send(x, axis, pairs):
    return lax.ppermute(x, axis, pairs)


def from_offset(x, frames, offset):
    return send(
        x, "frame", [(i + offset, i) for i in range(frames) if 0 <= i + offset < frames]
    )


def wait(x, name, done):
    return after(x, *(done[n] for n in BARS.get(name, ())))


def early_hops(x, frames, kind, done):
    if frames != 8:
        return [from_offset(x, frames, o) for o in offsets_for(frames)[1:-2]]
    hops = []
    for name, pairs in (
        ("E1", [(i, i ^ 2) for i in range(frames)]),
        ("E2", [(i, i ^ 6) for i in (2, 3, 4, 5)]),
        ("X", [(i, i ^ 1) for i in range(frames)]),
    ):
        hops.append(send(wait(x, name + kind, done), "frame", pairs))
        done[name + kind] = hops[-1]
    return hops


def late_hops(x, hops, own, frames, kind, done):
    if frames != 8:
        return [from_offset(x, frames, o) for o in offsets_for(frames)[-2:]]
    outer, inner, _ = hops
    across = jnp.where((own == 2) | (own == 5), inner, outer)
    results = []
    for name, x, pairs in (
        ("F1", outer, [(i, i ^ 6) for i in (2, 3, 4, 5)]),
        ("F2", inner, [(i, i ^ 2) for i in (2, 3, 4, 5)]),
        ("D", across, [(i, i ^ 1) for i in (0, 2, 3, 4, 5, 7)]),
    ):
        results.append(send(wait(x, name + kind, done), "frame", pairs))
        done[name + kind] = results[-1]
    return results


def plan(own, frames):
    if frames != 8:
        held = [own + o for o in offsets_for(frames)]
        return held[:-2], held[-2:], ((0,), (1,)), own >= 0
    middle = (own >= 2) & (own <= 5)
    odd = lax.rem(own, 2)
    flip = 1 - 2 * odd
    low = lax.rem(lax.div(own, 2), 2)
    outer = own + 2 - 4 * low
    early = [own, outer, jnp.where(middle, own - 2 + 4 * low, -1), own + flip]
    late = [jnp.where(own >= 4, own - 4, own + 4), own - flip]
    return early, late, ((0, 1), (2,)), middle


def params():
    return pltpu.CompilerParams(vmem_limit_bytes=20 << 20)


VMEM = pl.BlockSpec(memory_space=pltpu.VMEM)
SMEM = pl.BlockSpec(memory_space=pltpu.SMEM)


def fill_bias(bias_ref, live_ref, held, frames):
    blocks = live_ref.shape[0]
    left = lax.broadcasted_iota(jnp.int32, (8, 2 * BLK), 1) < BLK
    for n, frame in enumerate(held):
        inside = (frame >= 0) & (frame < frames)
        base = jnp.where(inside, frame, 0) * blocks
        for b in range(blocks):
            for c in range(0, blocks, 2):
                one, two = (
                    jnp.where(inside & (live_ref[b, base + c + d] > 0), 0.0, DEAD).astype(F32)
                    for d in (0, 1)
                )
                at = n * blocks * BLK + c * BLK
                bias_ref[8 * b : 8 * b + 8, at : at + 2 * BLK] = jnp.where(left, one, two)


def scores_of(q, key, bias_ref, n):
    rows = q.shape[0]
    s = lax.dot_general(q, key, (((1,), (1,)), ((), ())), preferred_element_type=F32)
    if bias_ref is None:
        return s
    parts = []
    for b in range(rows // BLK):
        bias = bias_ref[8 * b : 8 * b + 8, n * rows : (n + 1) * rows]
        part = s[b * BLK : (b + 1) * BLK].reshape(BLK // 8, 8, rows) + bias[None]
        parts.append(part.reshape(BLK, rows))
    return jnp.concatenate(parts, 0)


def each_head(heads, body, unroll):
    def some(step, _):
        for n in range(unroll):
            h = step * unroll + n
            body(h, pl.ds(pl.multiple_of(h * HDIM, HDIM), HDIM))
        return 0

    lax.fori_loop(0, heads // unroll, some, 0)


def early_kernel(count, live_ref, q_ref, k_ref, v_ref, *rest):
    keys, values = (k_ref, *rest[:count]), (v_ref, *rest[count : 2 * count])
    sum_ref, peak_ref, total_ref, bias_ref = rest[2 * count :]
    frames = lax.axis_size("frame")
    held = plan(lax.axis_index("frame"), frames)[0]
    fill_bias(bias_ref, live_ref, held[1:], frames)

    def head(h, columns):
        q = q_ref[:, columns]
        scores = []
        for n, ref in enumerate(keys):
            scores.append(scores_of(q, ref[:, columns], bias_ref if n else None, n - 1))
        peak = jnp.max(functools.reduce(jnp.maximum, scores), axis=1, keepdims=True)
        acc = None
        total = None
        for s, ref in zip(scores, values):
            e = jnp.exp2((s - peak) * EXP_SCALE)
            total = e if total is None else total + e
            part = jnp.dot(e.astype(BF16), ref[:, columns], preferred_element_type=F32)
            acc = part if acc is None else acc + part
        sum_ref[:, columns] = acc
        peak_ref[:, columns] = jnp.broadcast_to(peak, acc.shape)
        total_ref[:, columns] = jnp.broadcast_to(
            jnp.sum(total, axis=1, keepdims=True), acc.shape
        )

    each_head(q_ref.shape[1] // HDIM, head, 2)


def early_attention(live_blocks, queries, keys, values, early_keys, early_values):
    rows, width = queries.shape
    count = len(early_keys)
    seen = rows * (count + 1)
    heads = width // HDIM
    return pl.pallas_call(
        functools.partial(early_kernel, count),
        out_shape=[jax.ShapeDtypeStruct((rows, width), F32)] * 3,
        in_specs=[SMEM] + [VMEM] * (3 + 2 * count),
        out_specs=[VMEM] * 3,
        scratch_shapes=[pltpu.VMEM((8 * rows // BLK, count * rows), F32)],
        compiler_params=params(),
        cost_estimate=LIGHT,
        name="early_attention",
    )(live_blocks, queries, keys, values, *early_keys, *early_values)


def pick(refs, group, columns, first):
    if len(group) == 1:
        return refs[group[0]][:, columns]
    one, two = (refs[g][:, columns] for g in group)
    return jnp.where(first, one, two)


def late_kernel(live_ref, q_ref, sum_ref, peak_ref, total_ref, *rest):
    keys, (weight_ref, scaled_ref, bias_ref) = rest[:-3], rest[-3:]
    frames = lax.axis_size("frame")
    _, held, groups, first = plan(lax.axis_index("frame"), frames)
    rows = q_ref.shape[0]
    seen = rows * len(groups)
    fill_bias(bias_ref, live_ref, held, frames)

    def head(h, columns):
        q = q_ref[:, columns]
        scores = [
            scores_of(q, pick(keys, group, columns, first), bias_ref, n)
            for n, group in enumerate(groups)
        ]
        before = peak_ref[:, columns]
        peak = jnp.max(functools.reduce(jnp.maximum, scores), axis=1, keepdims=True)
        peak = jnp.maximum(before, jnp.broadcast_to(peak, before.shape))
        expos = []
        for s in scores:
            for c in range(0, rows, HDIM):
                expos.append(jnp.exp2((s[:, c : c + HDIM] - peak) * EXP_SCALE))
        total = jnp.sum(functools.reduce(jnp.add, expos), axis=1, keepdims=True)
        shrink = jnp.exp2((before - peak) * EXP_SCALE)
        over = 1.0 / (total_ref[:, columns] * shrink + jnp.broadcast_to(total, before.shape))
        for n, e in enumerate(expos):
            at = pl.multiple_of(h * seen + n * HDIM, HDIM)
            weight_ref[:, pl.ds(at, HDIM)] = (e * over).astype(BF16)
        scaled_ref[:, columns] = sum_ref[:, columns] * (shrink * over)

    each_head(q_ref.shape[1] // HDIM, head, 2)


def late_weights(live_blocks, queries, sums, peaks, totals, late_keys, places):
    rows, width = queries.shape
    heads = width // HDIM
    seen = rows * places
    return pl.pallas_call(
        late_kernel,
        out_shape=[
            jax.ShapeDtypeStruct((rows, heads * seen), BF16),
            jax.ShapeDtypeStruct((rows, width), F32),
        ],
        in_specs=[SMEM] + [VMEM] * (4 + len(late_keys)),
        out_specs=[VMEM] * 2,
        scratch_shapes=[pltpu.VMEM((8 * rows // BLK, seen), F32)],
        compiler_params=params(),
        cost_estimate=LIGHT,
        name="late_weights",
    )(live_blocks, queries, sums, peaks, totals, *late_keys)


def multiply(a_ref, w_ref, out_ref, *parts):
    columns = w_ref.shape[1] // lax.axis_size("head")
    base = 0
    for bit, start, width in parts:
        group = lax.axis_index("head") ^ bit
        for n in range(0, width, 2 * HDIM):
            step = min(2 * HDIM, width - n)
            at = pl.ds(pl.multiple_of(group * columns + (start + n), HDIM), step)
            out_ref[:, base + n : base + n + step] = jnp.dot(
                a_ref[...], w_ref[:, at], preferred_element_type=F32
            ).astype(BF16)
        base += width


def add_values(acc, weights_ref, values, group, first, h, n, places):
    rows = weights_ref.shape[0]
    value = pick(values, group, slice(h * HDIM, (h + 1) * HDIM), first)
    at = (h * places + n) * rows
    return acc + jnp.dot(weights_ref[:, at : at + rows], value, preferred_element_type=F32)


def second_place_kernel(scaled_ref, weights_ref, value_ref, out_ref):
    _, _, groups, first = plan(lax.axis_index("frame"), lax.axis_size("frame"))
    for h in range(scaled_ref.shape[1] // HDIM):
        columns = slice(h * HDIM, (h + 1) * HDIM)
        out_ref[:, columns] = add_values(
            scaled_ref[:, columns], weights_ref, (value_ref,), (0,), first, h, 1, len(groups)
        )


def second_place(scaled, weights, value):
    return pl.pallas_call(
        second_place_kernel,
        out_shape=jax.ShapeDtypeStruct(scaled.shape, F32),
        in_specs=[VMEM] * 3,
        out_specs=VMEM,
        compiler_params=params(),
        cost_estimate=LIGHT,
        name="second_place",
    )(scaled, weights, value)


def first_project_kernel(count, scaled_ref, weights_ref, *rest):
    values = rest[:count]
    w_ref, out_ref, att_ref = rest[count:]
    _, _, groups, first = plan(lax.axis_index("frame"), lax.axis_size("frame"))
    for h in range(scaled_ref.shape[1] // HDIM):
        columns = slice(h * HDIM, (h + 1) * HDIM)
        acc = add_values(
            scaled_ref[:, columns], weights_ref, values, groups[0], first, h, 0, len(groups)
        )
        att_ref[:, columns] = acc.astype(BF16)
    multiply(att_ref, w_ref, out_ref, (3, 0, out_ref.shape[1]))


def first_project(scaled, weights, late_values, weight, columns):
    rows, width = scaled.shape
    return pl.pallas_call(
        functools.partial(first_project_kernel, len(late_values)),
        out_shape=[
            jax.ShapeDtypeStruct((rows, columns), BF16),
            jax.ShapeDtypeStruct((rows, width), BF16),
        ],
        in_specs=[VMEM] * (3 + len(late_values)),
        out_specs=[VMEM] * 2,
        compiler_params=params(),
        cost_estimate=LIGHT,
        name="first_project",
    )(scaled, weights, *late_values, weight)


def project_kernel(outputs, a_ref, w_ref, *outs):
    for parts, out_ref in zip(outputs, outs):
        multiply(a_ref, w_ref, out_ref, *parts)


def project(attended, weight, *outputs):
    rows = attended.shape[0]
    return pl.pallas_call(
        functools.partial(project_kernel, outputs),
        out_shape=[
            jax.ShapeDtypeStruct((rows, sum(width for _, _, width in parts)), BF16)
            for parts in outputs
        ],
        in_specs=[VMEM] * 2,
        out_specs=[VMEM] * len(outputs),
        compiler_params=params(),
        cost_estimate=LIGHT,
        name="project",
    )(attended, weight)


def after(x, *others):
    return lax.optimization_barrier((x, *others))[0] if others else x


def on_device(queries, key_vectors, value_vectors, live_blocks, out_weight):
    frames = lax.axis_size("frame")
    own = lax.axis_index("frame")

    done = {}
    early_keys = early_hops(key_vectors, frames, "K", done)
    early_values = early_hops(value_vectors, frames, "V", done)
    late_keys = late_hops(key_vectors, early_keys, own, frames, "K", done)
    held_queries = wait(queries, "S", done) if frames == 8 else queries
    sums, peaks, totals = early_attention(
        live_blocks, held_queries, key_vectors, value_vectors, early_keys, early_values
    )
    done["S"] = sums
    late_values = late_hops(value_vectors, early_values, own, frames, "V", done)
    places = 2
    weights, scaled = late_weights(
        live_blocks, queries, sums, peaks, totals, late_keys, places
    )

    swap = lambda x, bit: send(x, "head", [(g, g ^ bit) for g in range(4)])
    add = lambda a, b: (a.astype(F32) + b.astype(F32)).astype(BF16)
    columns = out_weight.shape[1] // lax.axis_size("head")
    cut = columns // 2
    rest = columns - cut
    scaled = second_place(scaled, weights, late_values[-1])
    sibling_a, attended = first_project(scaled, weights, late_values[:-1], out_weight, cut)
    sibling_b, mine_a = project(attended, out_weight, ((3, cut, rest),), ((2, 0, cut),))
    crossed_a = add(mine_a, swap(sibling_a, 1))
    far_a = swap(crossed_a, 2)
    sibling_b = swap(after(sibling_b, crossed_a), 1)
    (mine_b,) = project(after(attended, crossed_a), out_weight, ((2, cut, rest),))
    crossed_b = add(mine_b, sibling_b)
    far_b = swap(crossed_b, 2)
    bounds = [0, 4 * HDIM, 8 * HDIM, columns]
    *near, total = project(
        after(attended, crossed_b), out_weight,
        *(((1, p, q - p),) for p, q in zip(bounds[:-1], bounds[1:])), ((0, 0, columns),),
    )
    near = jnp.concatenate([swap(part, 1) for part in near], 1)
    total = total.astype(F32) + near.astype(F32)
    far = jnp.concatenate([far_a, far_b], 1)
    return (total + far.astype(F32)).astype(BF16)


def solution(mesh):
    placed = (
        P("frame", "head"),
        P("frame", "head"),
        P("frame", "head"),
        P("frame", None),
        P("head", None),
    )
    return jax.shard_map(
        on_device, mesh=mesh, in_specs=placed, out_specs=P("frame", "head"), check_vma=False
    )
```

```python
import functools
import math

import jax
import jax.numpy as jnp
from jax import lax
from jax.experimental import pallas as pl
from jax.experimental.pallas import tpu as pltpu
from jax.sharding import PartitionSpec as P

HDIM = 128
BLK = 64
EXP_SCALE = math.log2(math.e) / math.sqrt(HDIM)
DEAD = -1e30
BARS = {'XV': ('E1K', 'XK'), 'F1K': ('E2K', 'E1V'), 'F1V': ('S',), 'DV': ('XV',)}
F32 = jnp.float32
BF16 = jnp.bfloat16
LIGHT = pl.CostEstimate(flops=0, bytes_accessed=0, transcendentals=0)


def offsets_for(frames):
    result = [0]
    step = 1
    while step <= frames // 2:
        result.append(step)
        result.append(-step)
        step = step * 2
    return result


def send(x, axis, pairs):
    return lax.ppermute(x, axis, pairs)


def from_offset(x, frames, offset):
    return send(
        x, "frame", [(i + offset, i) for i in range(frames) if 0 <= i + offset < frames]
    )


def wait(x, name, done):
    return after(x, *(done[n] for n in BARS.get(name, ())))


def early_hops(x, frames, kind, done):
    if frames != 8:
        return [from_offset(x, frames, o) for o in offsets_for(frames)[1:-2]]
    hops = []
    for name, pairs in (
        ("E1", [(i, i ^ 2) for i in range(frames)]),
        ("E2", [(i, i ^ 6) for i in (2, 3, 4, 5)]),
        ("X", [(i, i ^ 1) for i in range(frames)]),
    ):
        hops.append(send(wait(x, name + kind, done), "frame", pairs))
        done[name + kind] = hops[-1]
    return hops


def late_hops(x, hops, own, frames, kind, done):
    if frames != 8:
        return [from_offset(x, frames, o) for o in offsets_for(frames)[-2:]]
    outer, inner, _ = hops
    across = jnp.where((own == 2) | (own == 5), inner, outer)
    results = []
    for name, x, pairs in (
        ("F1", outer, [(i, i ^ 6) for i in (2, 3, 4, 5)]),
        ("F2", inner, [(i, i ^ 2) for i in (2, 3, 4, 5)]),
        ("D", across, [(i, i ^ 1) for i in (0, 2, 3, 4, 5, 7)]),
    ):
        results.append(send(wait(x, name + kind, done), "frame", pairs))
        done[name + kind] = results[-1]
    return results


def plan(own, frames):
    if frames != 8:
        held = [own + o for o in offsets_for(frames)]
        return held[:-2], held[-2:], ((0,), (1,)), own >= 0
    middle = (own >= 2) & (own <= 5)
    odd = lax.rem(own, 2)
    flip = 1 - 2 * odd
    low = lax.rem(lax.div(own, 2), 2)
    outer = own + 2 - 4 * low
    early = [own, outer, jnp.where(middle, own - 2 + 4 * low, -1), own + flip]
    late = [jnp.where(own >= 4, own - 4, own + 4), own - flip]
    return early, late, ((0, 1), (2,)), middle


def params():
    return pltpu.CompilerParams(vmem_limit_bytes=20 << 20)


VMEM = pl.BlockSpec(memory_space=pltpu.VMEM)
SMEM = pl.BlockSpec(memory_space=pltpu.SMEM)


def fill_bias(bias_ref, live_ref, held, frames):
    blocks = live_ref.shape[0]
    left = lax.broadcasted_iota(jnp.int32, (8, 2 * BLK), 1) < BLK
    for n, frame in enumerate(held):
        inside = (frame >= 0) & (frame < frames)
        base = jnp.where(inside, frame, 0) * blocks
        for b in range(blocks):
            for c in range(0, blocks, 2):
                one, two = (
                    jnp.where(inside & (live_ref[b, base + c + d] > 0), 0.0, DEAD).astype(F32)
                    for d in (0, 1)
                )
                at = n * blocks * BLK + c * BLK
                bias_ref[8 * b : 8 * b + 8, at : at + 2 * BLK] = jnp.where(left, one, two)


def scores_of(q, key, bias_ref, n):
    rows = q.shape[0]
    s = lax.dot_general(q, key, (((1,), (1,)), ((), ())), preferred_element_type=F32)
    if bias_ref is None:
        return s
    parts = []
    for b in range(rows // BLK):
        bias = bias_ref[8 * b : 8 * b + 8, n * rows : (n + 1) * rows]
        part = s[b * BLK : (b + 1) * BLK].reshape(BLK // 8, 8, rows) + bias[None]
        parts.append(part.reshape(BLK, rows))
    return jnp.concatenate(parts, 0)


def each_head(heads, body, unroll):
    def some(step, _):
        for n in range(unroll):
            h = step * unroll + n
            body(h, pl.ds(pl.multiple_of(h * HDIM, HDIM), HDIM))
        return 0

    lax.fori_loop(0, heads // unroll, some, 0)


def early_kernel(count, live_ref, q_ref, k_ref, v_ref, *rest):
    keys, values = (k_ref, *rest[:count]), (v_ref, *rest[count : 2 * count])
    sum_ref, peak_ref, total_ref, bias_ref = rest[2 * count :]
    frames = lax.axis_size("frame")
    held = plan(lax.axis_index("frame"), frames)[0]
    fill_bias(bias_ref, live_ref, held[1:], frames)

    def head(h, columns):
        q = q_ref[:, columns]
        scores = []
        for n, ref in enumerate(keys):
            scores.append(scores_of(q, ref[:, columns], bias_ref if n else None, n - 1))
        peak = jnp.max(functools.reduce(jnp.maximum, scores), axis=1, keepdims=True)
        acc = None
        total = None
        for s, ref in zip(scores, values):
            e = jnp.exp2((s - peak) * EXP_SCALE)
            total = e if total is None else total + e
            part = jnp.dot(e.astype(BF16), ref[:, columns], preferred_element_type=F32)
            acc = part if acc is None else acc + part
        sum_ref[:, columns] = acc
        peak_ref[:, columns] = jnp.broadcast_to(peak, acc.shape)
        total_ref[:, columns] = jnp.broadcast_to(
            jnp.sum(total, axis=1, keepdims=True), acc.shape
        )

    each_head(q_ref.shape[1] // HDIM, head, 2)


def early_attention(live_blocks, queries, keys, values, early_keys, early_values):
    rows, width = queries.shape
    count = len(early_keys)
    seen = rows * (count + 1)
    heads = width // HDIM
    return pl.pallas_call(
        functools.partial(early_kernel, count),
        out_shape=[jax.ShapeDtypeStruct((rows, width), F32)] * 3,
        in_specs=[SMEM] + [VMEM] * (3 + 2 * count),
        out_specs=[VMEM] * 3,
        scratch_shapes=[pltpu.VMEM((8 * rows // BLK, count * rows), F32)],
        compiler_params=params(),
        cost_estimate=LIGHT,
        name="early_attention",
    )(live_blocks, queries, keys, values, *early_keys, *early_values)


def pick(refs, group, columns, first):
    if len(group) == 1:
        return refs[group[0]][:, columns]
    one, two = (refs[g][:, columns] for g in group)
    return jnp.where(first, one, two)


def late_kernel(live_ref, q_ref, sum_ref, peak_ref, total_ref, *rest):
    keys, (weight_ref, scaled_ref, bias_ref) = rest[:-3], rest[-3:]
    frames = lax.axis_size("frame")
    _, held, groups, first = plan(lax.axis_index("frame"), frames)
    rows = q_ref.shape[0]
    seen = rows * len(groups)
    fill_bias(bias_ref, live_ref, held, frames)

    def head(h, columns):
        q = q_ref[:, columns]
        scores = [
            scores_of(q, pick(keys, group, columns, first), bias_ref, n)
            for n, group in enumerate(groups)
        ]
        before = peak_ref[:, columns]
        peak = jnp.max(functools.reduce(jnp.maximum, scores), axis=1, keepdims=True)
        peak = jnp.maximum(before, jnp.broadcast_to(peak, before.shape))
        expos = []
        for s in scores:
            for c in range(0, rows, HDIM):
                expos.append(jnp.exp2((s[:, c : c + HDIM] - peak) * EXP_SCALE))
        total = jnp.sum(functools.reduce(jnp.add, expos), axis=1, keepdims=True)
        shrink = jnp.exp2((before - peak) * EXP_SCALE)
        over = 1.0 / (total_ref[:, columns] * shrink + jnp.broadcast_to(total, before.shape))
        for n, e in enumerate(expos):
            at = pl.multiple_of(h * seen + n * HDIM, HDIM)
            weight_ref[:, pl.ds(at, HDIM)] = (e * over).astype(BF16)
        scaled_ref[:, columns] = sum_ref[:, columns] * (shrink * over)

    each_head(q_ref.shape[1] // HDIM, head, 2)


def late_weights(live_blocks, queries, sums, peaks, totals, late_keys, places):
    rows, width = queries.shape
    heads = width // HDIM
    seen = rows * places
    return pl.pallas_call(
        late_kernel,
        out_shape=[
            jax.ShapeDtypeStruct((rows, heads * seen), BF16),
            jax.ShapeDtypeStruct((rows, width), F32),
        ],
        in_specs=[SMEM] + [VMEM] * (4 + len(late_keys)),
        out_specs=[VMEM] * 2,
        scratch_shapes=[pltpu.VMEM((8 * rows // BLK, seen), F32)],
        compiler_params=params(),
        cost_estimate=LIGHT,
        name="late_weights",
    )(live_blocks, queries, sums, peaks, totals, *late_keys)


def multiply(a_ref, w_ref, out_ref, *parts):
    columns = w_ref.shape[1] // lax.axis_size("head")
    base = 0
    for bit, start, width in parts:
        group = lax.axis_index("head") ^ bit
        for n in range(0, width, 2 * HDIM):
            step = min(2 * HDIM, width - n)
            at = pl.ds(pl.multiple_of(group * columns + (start + n), HDIM), step)
            out_ref[:, base + n : base + n + step] = jnp.dot(
                a_ref[...], w_ref[:, at], preferred_element_type=F32
            ).astype(BF16)
        base += width


def add_values(acc, weights_ref, values, group, first, h, n, places):
    rows = weights_ref.shape[0]
    value = pick(values, group, slice(h * HDIM, (h + 1) * HDIM), first)
    at = (h * places + n) * rows
    return acc + jnp.dot(weights_ref[:, at : at + rows], value, preferred_element_type=F32)


def second_place_kernel(scaled_ref, weights_ref, value_ref, out_ref):
    _, _, groups, first = plan(lax.axis_index("frame"), lax.axis_size("frame"))
    for h in range(scaled_ref.shape[1] // HDIM):
        columns = slice(h * HDIM, (h + 1) * HDIM)
        out_ref[:, columns] = add_values(
            scaled_ref[:, columns], weights_ref, (value_ref,), (0,), first, h, 1, len(groups)
        )


def second_place(scaled, weights, value):
    return pl.pallas_call(
        second_place_kernel,
        out_shape=jax.ShapeDtypeStruct(scaled.shape, F32),
        in_specs=[VMEM] * 3,
        out_specs=VMEM,
        compiler_params=params(),
        cost_estimate=LIGHT,
        name="second_place",
    )(scaled, weights, value)


def first_project_kernel(count, scaled_ref, weights_ref, *rest):
    values = rest[:count]
    w_ref, out_ref, att_ref = rest[count:]
    _, _, groups, first = plan(lax.axis_index("frame"), lax.axis_size("frame"))
    for h in range(scaled_ref.shape[1] // HDIM):
        columns = slice(h * HDIM, (h + 1) * HDIM)
        acc = add_values(
            scaled_ref[:, columns], weights_ref, values, groups[0], first, h, 0, len(groups)
        )
        att_ref[:, columns] = acc.astype(BF16)
    multiply(att_ref, w_ref, out_ref, (3, 0, out_ref.shape[1]))


def first_project(scaled, weights, late_values, weight, columns):
    rows, width = scaled.shape
    return pl.pallas_call(
        functools.partial(first_project_kernel, len(late_values)),
        out_shape=[
            jax.ShapeDtypeStruct((rows, columns), BF16),
            jax.ShapeDtypeStruct((rows, width), BF16),
        ],
        in_specs=[VMEM] * (3 + len(late_values)),
        out_specs=[VMEM] * 2,
        compiler_params=params(),
        cost_estimate=LIGHT,
        name="first_project",
    )(scaled, weights, *late_values, weight)


def project_kernel(outputs, a_ref, w_ref, *outs):
    for parts, out_ref in zip(outputs, outs):
        multiply(a_ref, w_ref, out_ref, *parts)


def project(attended, weight, *outputs):
    rows = attended.shape[0]
    return pl.pallas_call(
        functools.partial(project_kernel, outputs),
        out_shape=[
            jax.ShapeDtypeStruct((rows, sum(width for _, _, width in parts)), BF16)
            for parts in outputs
        ],
        in_specs=[VMEM] * 2,
        out_specs=[VMEM] * len(outputs),
        compiler_params=params(),
        cost_estimate=LIGHT,
        name="project",
    )(attended, weight)


def after(x, *others):
    return lax.optimization_barrier((x, *others))[0] if others else x


def on_device(queries, key_vectors, value_vectors, live_blocks, out_weight):
    frames = lax.axis_size("frame")
    own = lax.axis_index("frame")

    done = {}
    early_keys = early_hops(key_vectors, frames, "K", done)
    early_values = early_hops(value_vectors, frames, "V", done)
    late_keys = late_hops(key_vectors, early_keys, own, frames, "K", done)
    held_queries = wait(queries, "S", done) if frames == 8 else queries
    sums, peaks, totals = early_attention(
        live_blocks, held_queries, key_vectors, value_vectors, early_keys, early_values
    )
    done["S"] = sums
    late_values = late_hops(value_vectors, early_values, own, frames, "V", done)
    places = 2
    weights, scaled = late_weights(
        live_blocks, queries, sums, peaks, totals, late_keys, places
    )

    swap = lambda x, bit: send(x, "head", [(g, g ^ bit) for g in range(4)])
    add = lambda a, b: (a.astype(F32) + b.astype(F32)).astype(BF16)
    columns = out_weight.shape[1] // lax.axis_size("head")
    cut = 4 * HDIM
    rest = columns - cut
    scaled = second_place(scaled, weights, late_values[-1])
    sibling_a, attended = first_project(scaled, weights, late_values[:-1], out_weight, cut)
    sibling_b, mine_a = project(attended, out_weight, ((3, cut, rest),), ((2, 0, cut),))
    crossed_a = add(mine_a, swap(sibling_a, 1))
    fars = [swap(crossed_a, 2)]
    sibling_b = swap(after(sibling_b, crossed_a), 1)
    (mine_b,) = project(after(attended, crossed_a), out_weight, ((2, cut, rest),))
    crossed_b = add(mine_b, sibling_b)
    cuts = [0, 3 * HDIM, rest]
    fars += [swap(crossed_b[:, p:q], 2) for p, q in zip(cuts[:-1], cuts[1:])]
    bounds = [0, 3 * HDIM, 6 * HDIM, 8 * HDIM, columns]
    *near, total = project(
        after(attended, crossed_b), out_weight,
        *(((1, p, q - p),) for p, q in zip(bounds[:-1], bounds[1:])), ((0, 0, columns),),
    )
    near = jnp.concatenate([swap(part, 1) for part in near], 1)
    total = total.astype(F32) + near.astype(F32)
    return (total + jnp.concatenate(fars, 1).astype(F32)).astype(BF16)


def solution(mesh):
    placed = (
        P("frame", "head"),
        P("frame", "head"),
        P("frame", "head"),
        P("frame", None),
        P("head", None),
    )
    return jax.shard_map(
        on_device, mesh=mesh, in_specs=placed, out_specs=P("frame", "head"), check_vma=False
    )
```
